32 devices in a mesh: dp: 8 (over z, x), tensor: 4 (over y, core).
Axes of the slice: x: 2, y: 2, z: 4, core: 2. Of those that a mesh axis runs over, the one named last changes fastest.
Arguments:
- inputs: bfloat16 [580, 24, 1024], P('tensor', 'dp'), may hold values from -6 to 6
- wqkv: bfloat16 [1024, 3, 1024], P('dp', None, 'tensor'), may hold values from -0.1875 to 0.1875
- qv_bias: bfloat16 [2, 16, 64], P(None, 'tensor', 'dp'), may hold values from -0.625 to 0.625
- wo: bfloat16 [1024, 1024], P('tensor', 'dp'), may hold values from -1.5 to 1.5
- w1: bfloat16 [1024, 4096], P('dp', 'tensor'), may hold values from -0.1875 to 0.1875
- b1: bfloat16 [64, 64], P('tensor', 'dp'), may hold values from -1.25 to 1.25
- w2: bfloat16 [4096, 1024], P('tensor', 'dp'), may hold values from -0.09375 to 0.09375
- gains: bfloat16 [2, 1024], P(None, 'dp'), may hold values from 0.25 to 1.75
- shifts: bfloat16 [4, 1024], P(None, 'dp'), may hold values from -1.25 to 1.25
- cotangent: bfloat16 [580, 24, 1024], P('tensor', 'dp'), may hold values from -8 to 8
- span_lengths: int32 [4], replicated, may hold values from 1 to 145, 577 in all
Outputs:
- outputs: bfloat16 [580, 24, 1024], P('tensor', 'dp')
- grad_inputs: float32 [580, 24, 1024], P('tensor', 'dp')
- grad_wqkv: float32 [1024, 3, 1024], P('dp', None, 'tensor')
- grad_qv_bias: float32 [2, 16, 64], P(None, 'tensor', 'dp')
- grad_wo: float32 [1024, 1024], P('tensor', 'dp')
- grad_w1: float32 [1024, 4096], P('dp', 'tensor')
- grad_b1: float32 [64, 64], P('tensor', 'dp')
- grad_w2: float32 [4096, 1024], P('tensor', 'dp')
- grad_gains: float32 [2, 1024], P(None, 'dp')
- grad_shifts: float32 [4, 1024], P(None, 'dp')
The draws below stay inside these ranges and needn't reach their ends.
Inputs may be any that keep to these rules, and one draw needn't show every extreme that they name: Rank r of tensor holds span_lengths[r] tokens of every image in its first slots; the lengths sum to 577 and one equals 145.
All inputs are finite; a program needn't handle non-finite values.
Results may differ from the reference program's by a relative error of at most 0.017.
Values may be sent and summed in bfloat16 or wider, within the bound.
No kernel may reach another device: no remote copies, remote signals or barrier semaphores. Data moves between devices by JAX's collectives and lax.ppermute only.
A program may use at most 192 MiB of HBM per device.

```python
import math
import jax
import jax.numpy as jnp
import numpy as np
from jax import lax

D = 1024
HEADS = 16
HD = 64
FF = 4096
SEQ = 577
IMG_DEV = 3
SPAN = 145
SLOTS = 580
IMAGES = 24
N_TENSOR = 4


def with_spikes(values, stream_key, source, target, blocks, factor):
    owner, partner = [(jnp.arange(values.shape[position]) // (values.shape[position] // blocks)).reshape([-1 if axis == position else 1 for axis in range(values.ndim)]) for position in (source, target)]
    chosen = jax.random.permutation(stream_key, blocks)[partner]
    strong = (owner == chosen) | (owner == (partner + blocks // 2) % blocks)
    return jnp.where(strong, factor * values, values)


def block_levels(rng, shape, cuts, low, high):
    factor_of, own = 1.0, jax.random.fold_in(rng, 6)
    for axis_at, parts in cuts:
        draws = jnp.exp(jax.random.uniform(jax.random.fold_in(own, axis_at), (parts,), jnp.float32, low / len(cuts), high / len(cuts)))
        factor_of = factor_of * jnp.repeat(draws, shape[axis_at] // parts).reshape([-1 if axis == axis_at else 1 for axis in range(len(shape))])
    return factor_of


def profile(count, total, bound, slope):
    weights = [(1 << 20) // math.isqrt(grade ** slope) + 1 for grade in range(2, count + 1)]
    spare, given = total - bound - (count - 1), [1] * (count - 1)
    while spare > 0:
        candidates = [i for i in range(count - 1) if given[i] < bound]
        mass, budget = sum([weights[i] for i in candidates]), spare
        for i in candidates:
            addition = min(bound - given[i], max(1, budget * weights[i] // mass), spare)
            given[i] = given[i] + addition
            spare = spare - addition
    return np.array([bound] + given)


def ragged_sizes(rng, number_of, total, limit, slope):
    if number_of == 2:
        one = jax.random.randint(rng, (), max(1, total - limit), min(limit, total - 1) + 1)
        return jnp.stack([one, total - one])
    sizes = jnp.asarray(profile(number_of, total, limit, slope), jnp.int32)
    pairs = (number_of - 1) // 2
    source_of, receiver = sizes[1:1 + 2 * pairs:2], sizes[2:2 + 2 * pairs:2]
    margin = jnp.minimum(source_of - 1, limit - receiver)
    passed = jax.random.randint(jax.random.fold_in(rng, 1), (pairs,), 0, 1 << 20) % (margin + 1)
    sizes = sizes.at[1:1 + 2 * pairs:2].set(source_of - passed).at[2:2 + 2 * pairs:2].set(receiver + passed)
    return sizes[jax.random.permutation(jax.random.fold_in(rng, 2), number_of)]


def normal_values(own_key, shape, spread, most, pieces=(), kind=jnp.bfloat16):
    values = jax.random.normal(own_key, shape, jnp.float32) * spread
    if len(pieces) > 0:
        values = block_levels(own_key, shape, pieces, -0.22, 0.18) * values
    return jnp.clip(values, min=-most, max=most).astype(kind)


def gaussian_with(stream_key, dims, deviation, most, pieces, heavy, held_as=jnp.bfloat16):
    values = deviation * jax.random.normal(stream_key, dims, jnp.float32)
    if pieces:
        values = values * block_levels(stream_key, dims, pieces, -0.22, 0.18)
    return jnp.clip(with_spikes(values, jax.random.fold_in(stream_key, 3), *heavy), -most, most).astype(held_as)


def setup_inputs(seed: int = 0) -> dict:
    keys = jax.random.split(jax.random.key(seed), 12)
    return {
        "inputs": normal_values(keys[0], (SLOTS, IMAGES, D), 1.0, 6.0, ((0, 4), (1, 8))),
        "wqkv": normal_values(keys[1], (D, 3, D), D ** -0.5, 0.1875, ((0, 8), (2, 4))),
        "qv_bias": normal_values(keys[2], (2, HEADS, HD), 0.1, 0.625, ((1, 4), (2, 8))),
        "wo": normal_values(keys[3], (D, D), (D // 64) ** -0.5, 1.5, ((0, 4), (1, 8))),
        "w1": normal_values(keys[4], (D, FF), D ** -0.5, 0.1875, ((0, 8), (1, 4))),
        "b1": normal_values(keys[5], (FF // HD, HD), 0.2, 1.25, ((0, 4), (1, 8))),
        "w2": normal_values(keys[6], (FF, D), FF ** -0.5, 0.09375, ((0, 4), (1, 8))),
        "gains": jnp.clip(1.0 + 0.15 * jax.random.normal(keys[7], (2, D), jnp.float32), 0.25, 1.75).astype(jnp.bfloat16),
        "shifts": normal_values(keys[8], (4, D), 0.2, 1.25, ((1, 8),)),
        "cotangent": gaussian_with(keys[9], (SLOTS, IMAGES, D), 1.0, 8.0, ((0, 4), (1, 8)), (1, 2, 8, 2.0)),
        "span_lengths": ragged_sizes(keys[10], N_TENSOR, SEQ, SPAN, 0).astype(jnp.int32),
    }


@jax.custom_vjp
def low(v):
    return lax.optimization_barrier(v.astype(jnp.bfloat16)).astype(jnp.float32)

@jax.custom_vjp
def low_back(v):
    return v

def low_keep(v):
    return (low(v), None)

def low_pass(kept, grad):
    return (grad,)

def back_keep(v):
    return (v, None)

def back_low(kept, grad):
    return (low(grad),)
low.defvjp(low_keep, low_pass)
low_back.defvjp(back_keep, back_low)
norm_eps = 1e-06
masked_score = -1e+30

def layer_norm(values, gain, shift):
    row_mean = lax.optimization_barrier(jnp.mean(values, axis=-1, keepdims=True))
    centered = values - row_mean
    row_var = lax.optimization_barrier(jnp.mean(centered * centered, axis=-1, keepdims=True))
    return centered * lax.rsqrt(row_var + norm_eps) * gain + shift

def gelu_exact(values):
    return jax.nn.gelu(values, approximate=False)

def block_forward(inputs, wqkv, qv_bias, wo, w1, b1, w2, gains, shifts, valid):
    highest = lax.Precision.HIGHEST
    slots, images, width = inputs.shape
    heads = qv_bias.shape[1]
    head_dim = qv_bias.shape[2]
    h1 = low(layer_norm(inputs, gains[0], shifts[0]))
    bias_rows = qv_bias.reshape(2, width)
    qkv_bias = jnp.stack([bias_rows[0], jnp.zeros_like(bias_rows[0]), bias_rows[1]])
    qkv = jnp.einsum('sbd,dcn->sbcn', h1, wqkv, precision=highest) + qkv_bias
    qkv = low(low_back(qkv))
    queries = qkv[:, :, 0].reshape(slots, images, heads, head_dim)
    keys_all = qkv[:, :, 1].reshape(slots, images, heads, head_dim)
    values_all = qkv[:, :, 2].reshape(slots, images, heads, head_dim)
    scores = low_back(jnp.einsum('sbhe,tbhe->bhst', queries, keys_all, precision=highest) * head_dim ** (-0.5))
    scores = jnp.where(valid[None, None, None, :] > 0.5, scores, masked_score)
    exps = jnp.exp(scores - lax.optimization_barrier(jnp.max(scores, axis=-1, keepdims=True)))
    probs = low(exps / lax.optimization_barrier(jnp.sum(exps, axis=-1, keepdims=True)))
    attended = jnp.einsum('bhst,tbhe->sbhe', probs, values_all, precision=highest).reshape(slots, images, width)
    attended = low(low_back(attended))
    mid = inputs + low_back(jnp.einsum('sbn,nd->sbd', attended, wo, precision=highest)) + shifts[2]
    h2 = low(layer_norm(mid, gains[1], shifts[1]))
    pre_act = low_back(jnp.einsum('sbd,df->sbf', h2, w1, precision=highest) + b1.reshape(-1))
    activation = low(gelu_exact(pre_act))
    result = mid + low_back(jnp.einsum('sbf,fd->sbd', activation, w2, precision=highest)) + shifts[3]
    return result * valid[:, None, None]

def reference(inputs, wqkv, qv_bias, wo, w1, b1, w2, gains, shifts, cotangent, span_lengths):
    slots = N_TENSOR * SPAN
    row_ids = jnp.arange(slots, dtype=jnp.int32)
    valid = (row_ids % SPAN < span_lengths[row_ids // SPAN]).astype(jnp.float32)
    params = tuple((weight.astype(jnp.float32) for weight in (wqkv, qv_bias, wo, w1, b1, w2, gains, shifts)))
    groups = IMAGES // IMG_DEV
    grouped_in = jnp.transpose(inputs.astype(jnp.float32).reshape(slots, groups, IMG_DEV, D), (1, 0, 2, 3))
    grouped_cot = jnp.transpose(cotangent.astype(jnp.float32).reshape(slots, groups, IMG_DEV, D), (1, 0, 2, 3))

    def forward(values, *weights):
        return block_forward(values, *weights, valid)

    def group_step(totals, item):
        group_in, group_cot = item
        result, back = jax.vjp(forward, group_in, *params)
        grads = back(group_cot)
        totals = tuple((total + grad for total, grad in zip(totals, grads[1:])))
        return (totals, (result, grads[0]))
    start_totals = tuple((jnp.zeros_like(weight) for weight in params))
    totals, (results, in_grads) = lax.scan(group_step, start_totals, (grouped_in, grouped_cot))
    outputs = jnp.transpose(results, (1, 0, 2, 3)).reshape(slots, IMAGES, D).astype(jnp.bfloat16)
    grad_inputs = jnp.transpose(in_grads, (1, 0, 2, 3)).reshape(slots, IMAGES, D)
    return (outputs, grad_inputs, totals[0], totals[1], totals[2], totals[3], totals[4], totals[5], totals[6], totals[7])
```

```python
import functools

import jax
import jax.numpy as jnp
from jax import lax
from jax.experimental import pallas as pl
from jax.experimental.pallas import tpu as pltpu
from jax.sharding import PartitionSpec as P

norm_eps = 1e-06
masked_score = -1e30
f32 = jnp.float32
bf16 = jnp.bfloat16
NT = (((1,), (1,)), ((), ()))
TN = (((0,), (0,)), ((), ()))
NN = (((1,), (0,)), ((), ()))


def dot(a, b, dims=NN):
    return lax.dot_general(a, b, dims, preferred_element_type=f32)


def up(size, step):
    return -(-size // step) * step


def call(kernel, out_shape, *args, vmem=40, flops=0, nbytes=0, scalars=0, **kw):
    if "grid" not in kw:
        kw["in_specs"] = [
            pl.BlockSpec(memory_space=pltpu.SMEM if i < scalars else pltpu.VMEM)
            for i in range(len(args))
        ]
        kw["out_specs"] = jax.tree.map(
            lambda _: pl.BlockSpec(memory_space=pltpu.VMEM), out_shape
        )
    return pl.pallas_call(
        kernel,
        out_shape=out_shape,
        compiler_params=pltpu.CompilerParams(vmem_limit_bytes=vmem << 20),
        cost_estimate=pl.CostEstimate(flops=flops, bytes_accessed=nbytes, transcendentals=0),
        **kw,
    )(*args)


def sds(shape, dtype):
    return jax.ShapeDtypeStruct(shape, dtype)


def hop(x, axis, k):
    size = lax.axis_size(axis)
    return lax.ppermute(x, axis, [(i, i ^ k) for i in range(size)])


def gather_tokens(x):
    near = jnp.concatenate([x, hop(x, "tensor", 2)], axis=0)
    return near, hop(near, "tensor", 1)


def scatter_tokens(keep, send):
    rows = keep.shape[0] // 2
    got = hop(send, "tensor", 1)
    far = (keep[rows:].astype(f32) + got[rows:].astype(f32)).astype(bf16)
    far = hop(far, "tensor", 2)
    return keep[:rows].astype(f32) + got[:rows].astype(f32) + far.astype(f32)


def dp_blocks(x):
    near = {0: x}
    for k in (2, 4, 6):
        near[k] = hop(x, "dp", k)
    blocks = dict(near)
    for k in (0, 2, 4, 6):
        blocks[k + 1] = hop(near[k], "dp", 1)
    return [blocks[k] for k in range(8)]


def dp_reduce(block):
    sums = {}
    for k in (6, 4, 2, 0):
        sums[k] = block(k).astype(f32) + hop(block(k + 1).astype(bf16), "dp", 1).astype(f32)
    total = sums[0]
    for k in (6, 4, 2):
        total = total + hop(sums[k].astype(bf16), "dp", k).astype(f32)
    return total


def dp_reduce_f32(block):
    sums = {}
    for k in (6, 4, 2, 0):
        sums[k] = block(k) + hop(block(k + 1), "dp", 1)
    total = sums[0]
    for k in (6, 4, 2):
        total = total + hop(sums[k], "dp", k)
    return total


def place_rows(index, *refs):
    *blocks, out, extra = refs
    count, rows = out.shape[0], out.shape[1] // 8
    for k, block in enumerate(blocks):
        at = index[0] ^ k
        for c in range(count):
            out[c, pl.ds(pl.multiple_of(at * rows, 16), rows), :] = block[
                c * rows : (c + 1) * rows, :
            ]
        extra[at] = block[count * rows :, :]


def place_columns(index, *refs):
    *blocks, out = refs
    for k, block in enumerate(blocks):
        at = index[0] ^ k
        out[:, pl.ds(pl.multiple_of(at * 128, 128), 128)] = block[...]


def place_plain(index, *refs):
    *blocks, out = refs
    rows = out.shape[0] // 8
    for k, block in enumerate(blocks):
        at = index[0] ^ k
        out[pl.ds(pl.multiple_of(at * rows, 16), rows), :] = block[...]


def norm_rows(x, gain, shift):
    mean = jnp.mean(x, axis=-1, keepdims=True)
    centered = x - mean
    var = jnp.mean(centered * centered, axis=-1, keepdims=True)
    return centered * lax.rsqrt(var + norm_eps) * gain + shift


def attention_kernel(near, far, wqkv, bias, gs, kmask, h1, qkv, att, lse):
    half = near.shape[0]
    rows = 2 * half
    width = wqkv.shape[2]
    for i, ref in enumerate((near, far)):
        x = ref[...].astype(f32)
        h1[i * half : (i + 1) * half, :] = norm_rows(x, gs[0:1, :], gs[1:2, :]).astype(bf16)
    for c in range(3):
        out = dot(h1[...], wqkv[c])
        if c != 1:
            out = out + bias[c // 2 : c // 2 + 1, :]
        out = out.astype(bf16)
        if c == 0:
            out = out * bf16(0.125)
        qkv[:, c * width : (c + 1) * width] = out
    lane = lax.broadcasted_iota(jnp.int32, (1, 128), 1)
    lane_f = lane
    lse_parts = [jnp.zeros((half, 128), f32) for _ in range(2)]
    for p in range(width // 128):
        keys = qkv[:, width + p * 128 : width + (p + 1) * 128]
        vals = qkv[:, 2 * width + p * 128 : 2 * width + (p + 1) * 128]
        outs = [jnp.zeros((half, 128), f32) for _ in range(2)]
        for h in range(2):
            mine = (lane >= 64 * h) & (lane < 64 * h + 64)
            k_h = jnp.where(mine, keys, bf16(0))
            v_h = jnp.where(mine, vals, bf16(0))
            for b in range(2):
                q = qkv[b * half : (b + 1) * half, p * 128 : (p + 1) * 128]
                s = dot(q, k_h, NT) + kmask[...]
                top = jnp.max(s, axis=-1, keepdims=True)
                e = jnp.exp(s - top)
                total = jnp.sum(e, axis=-1, keepdims=True)
                outs[b] = outs[b] + dot(e.astype(bf16), v_h) / total
                lse_parts[b] = jnp.where(
                    lane_f == 2 * p + h, top + jnp.log(total), lse_parts[b]
                )
        for b in range(2):
            att[b * half : (b + 1) * half, p * 128 : (p + 1) * 128] = outs[b].astype(bf16)
    for b in range(2):
        lse[b * half : (b + 1) * half, :] = lse_parts[b]


def attention_back_kernel(
    near, far, wo, wqkv, qkv, att, lse, kmask, dqkv, dh_keep, dh_send, d_att
):
    half = near.shape[0]
    rows = 2 * half
    width = wo.shape[0]
    for i, ref in enumerate((near, far)):
        d_att[i * half : (i + 1) * half, :] = dot(ref[...], wo[...], NT).astype(bf16)
    prod = d_att[...].astype(f32) * att[...].astype(f32)
    heads = width // 64
    pick_d = (
        lax.broadcasted_iota(jnp.int32, (8, width), 1) // 64
        == lax.broadcasted_iota(jnp.int32, (8, width), 0)
    ).astype(f32)
    pick_l = (
        lax.broadcasted_iota(jnp.int32, (8, 128), 1)
        == lax.broadcasted_iota(jnp.int32, (8, 128), 0)
    ).astype(f32)
    row_dot = lax.dot_general(
        pick_d, prod, NT, precision=lax.Precision.HIGHEST, preferred_element_type=f32
    )
    row_lse = lax.dot_general(
        pick_l, lse[...], NT, precision=lax.Precision.HIGHEST, preferred_element_type=f32
    )
    lane = lax.broadcasted_iota(jnp.int32, (1, 128), 1)
    for p in range(width // 128):
        cols = slice(p * 128, (p + 1) * 128)
        q = qkv[:, p * 128 : (p + 1) * 128]
        d_o = d_att[:, cols]
        dq = jnp.zeros((rows, 128), f32)
        for b in range(2):
            block = slice(b * half, (b + 1) * half)
            keys = qkv[block, width + p * 128 : width + (p + 1) * 128]
            vals = qkv[block, 2 * width + p * 128 : 2 * width + (p + 1) * 128]
            dk = jnp.zeros((half, 128), f32)
            dv = jnp.zeros((half, 128), f32)
            for h in range(2):
                mine = (lane >= 64 * h) & (lane < 64 * h + 64)
                k_h = jnp.where(mine, keys, bf16(0))
                v_h = jnp.where(mine, vals, bf16(0))
                at = 2 * p + h
                s = dot(k_h, q, NT) + kmask[block, :]
                probs = jnp.exp(s - row_lse[at : at + 1, :])
                d_p = dot(v_h, d_o, NT)
                d_s = (probs * (d_p - row_dot[at : at + 1, :])).astype(bf16)
                dv = dv + dot(probs.astype(bf16), jnp.where(mine, d_o, bf16(0)))
                dk = dk + dot(d_s, jnp.where(mine, q, bf16(0)))
                dq = dq + dot(d_s, k_h, TN)
            dqkv[block, width + p * 128 : width + (p + 1) * 128] = dk.astype(bf16)
            dqkv[block, 2 * width + p * 128 : 2 * width + (p + 1) * 128] = dv.astype(bf16)
        dqkv[:, p * 128 : (p + 1) * 128] = (dq * 0.125).astype(bf16)
    for i, ref in enumerate((dh_keep, dh_send)):
        block = slice(i * half, (i + 1) * half)
        total = dot(dqkv[block, 0:width], wqkv[0], NT)
        for c in (1, 2):
            total = total + dot(dqkv[block, c * width : (c + 1) * width], wqkv[c], NT)
        ref[...] = total.astype(bf16)


def gelu_parts(u):
    e = jnp.exp(-0.5 * u * u)
    t = 1.0 / (1.0 + (0.3275911 * 0.7071067811865476) * jnp.abs(u))
    poly = t * (
        0.5 * 0.254829592
        + t
        * (
            0.5 * -0.284496736
            + t * (0.5 * 1.421413741 + t * (0.5 * -1.453152027 + t * (0.5 * 1.061405429)))
        )
    )
    tail = poly * e
    phi_sum = jnp.where(u >= 0, 1.0 - tail, tail)
    return u * phi_sum, phi_sum + u * (e * 0.3989422804014327)


def mlp_kernel(
    near, far, dnear, dfar, w1, w2, b1, act, dpre, dh_keep, dh_send, y_keep, y_send, acc_d, acc_y
):
    step = pl.program_id(0)
    half = near.shape[0]
    for i, (h_ref, d_ref) in enumerate(((near, dnear), (far, dfar))):
        block = slice(i * half, (i + 1) * half)
        pre = dot(h_ref[...], w1[...]) + b1[...]
        d_act = dot(d_ref[...], w2[...], NT)
        value, slope = gelu_parts(pre)
        value = value.astype(bf16)
        grad = (d_act * slope).astype(bf16)
        act[block, :] = value
        dpre[block, :] = grad
        d_part = dot(grad, w1[...], NT)
        y_part = dot(value, w2[...])

        @pl.when(step == 0)
        def _():
            acc_d[block, :] = d_part
            acc_y[block, :] = y_part

        @pl.when(step > 0)
        def _():
            acc_d[block, :] += d_part
            acc_y[block, :] += y_part

    @pl.when(step == pl.num_programs(0) - 1)
    def _():
        dh_keep[...] = acc_d[0:half, :].astype(bf16)
        dh_send[...] = acc_d[half:, :].astype(bf16)
        y_keep[...] = acc_y[0:half, :].astype(bf16)
        y_send[...] = acc_y[half:, :].astype(bf16)


def norm_back(values, gain, grad):
    mean = jnp.mean(values, axis=-1, keepdims=True)
    centered = values - mean
    var = jnp.mean(centered * centered, axis=-1, keepdims=True)
    r = lax.rsqrt(var + norm_eps)
    xhat = centered * r
    f = grad * gain
    d_in = r * (
        f
        - jnp.mean(f, axis=-1, keepdims=True)
        - xhat * jnp.mean(f * xhat, axis=-1, keepdims=True)
    )
    return d_in, jnp.sum(grad * xhat, axis=0), jnp.sum(grad, axis=0)


def body(inputs, wqkv, qv_bias, wo, w1, b1, w2, gains, shifts, cotangent, span_lengths):
    slots, images, width_d = inputs.shape
    dp_size = lax.axis_size("dp")
    dp_index = lax.axis_index("dp")
    rank = lax.axis_index("tensor")
    rows = up(slots, 8)
    half, every = 2 * rows, 4 * rows
    width = wqkv.shape[2]
    heads, head_dim = qv_bias.shape[1], qv_bias.shape[2] * dp_size
    hidden = w1.shape[1]

    def apart(x):
        return jnp.pad(jnp.transpose(x, (1, 0, 2)), ((0, 0), (0, rows - slots), (0, 0)))

    x_own = apart(inputs)
    slot = jnp.arange(rows, dtype=jnp.int32)
    order = jnp.stack([rank, rank ^ 2, rank ^ 1, rank ^ 3])
    valid_all = (slot[None, :] < span_lengths[order][:, None]).reshape(every)
    valid_own = (slot < span_lengths[rank]).astype(f32)[:, None]
    kmask = jnp.where(valid_all, 0.0, masked_score).astype(f32)
    kmask_row, kmask_col = kmask[None, :], kmask[:, None]

    x_all = [gather_tokens(x_own[i]) for i in range(images)]

    index = dp_index.astype(jnp.int32)[None]
    if dp_size == 8:
        small = jnp.concatenate(
            [
                gains,
                shifts,
                b1.reshape(1, -1),
                jnp.pad(qv_bias.reshape(1, -1), ((0, 0), (0, 128 - qv_bias.size))),
            ]
        )
        first = jnp.concatenate(
            [
                jnp.transpose(wqkv, (1, 0, 2)).reshape(-1, width),
                jnp.pad(small, ((0, 8), (0, width - 128))),
            ]
        )
        wqkv_full, extra = call(
            place_rows,
            (sds((3, width_d, width), bf16), sds((8, 16, width), bf16)),
            index,
            *dp_blocks(first),
            scalars=1,
        )
        extra = extra[:, :8, :128].astype(f32)
        gs = jnp.transpose(extra[:, :6], (1, 0, 2)).reshape(6, width_d)
        b1_full = jnp.transpose(extra[:, 6].reshape(8, -1, 8), (1, 0, 2)).reshape(1, hidden)
        qvb_full = jnp.transpose(
            extra[:, 7, : qv_bias.size].reshape(8, 2, heads, -1), (1, 2, 0, 3)
        ).reshape(2, width)
        second = jnp.concatenate([wo, w2], axis=0)
        wide = call(
            place_columns,
            sds((second.shape[0], width_d), bf16),
            index,
            *dp_blocks(second),
            scalars=1,
        )
        wo_full, w2_full = wide[:width], wide[width:]
        w1_full = call(place_plain, sds((width_d, hidden), bf16), index, *dp_blocks(w1), scalars=1)
    else:
        wqkv_full = jnp.transpose(lax.all_gather(wqkv, "dp", axis=0, tiled=True), (1, 0, 2))
        wo_full = lax.all_gather(wo, "dp", axis=1, tiled=True)
        w1_full = lax.all_gather(w1, "dp", axis=0, tiled=True)
        w2_full = lax.all_gather(w2, "dp", axis=1, tiled=True)
        gs = lax.all_gather(jnp.concatenate([gains, shifts]), "dp", axis=1, tiled=True).astype(f32)
        b1_full = lax.all_gather(b1, "dp", axis=1, tiled=True).astype(f32).reshape(1, hidden)
        qvb_full = lax.all_gather(qv_bias, "dp", axis=2, tiled=True).astype(f32).reshape(2, width)
    gain1, gain2 = gs[0], gs[1]
    shift1, shift2, shift_o, shift_f = gs[2], gs[3], gs[4], gs[5]
    gs1 = jnp.stack([gain1, shift1])

    d_out = apart(cotangent).astype(f32) * valid_own
    d_out_b = d_out.astype(bf16)
    d_all = [gather_tokens(d_out_b[i]) for i in range(images)]

    kept = []
    mids, h2s = [], []
    for i in range(images):
        near, far = x_all[i]
        h1, qkv, att, lse = call(
            attention_kernel,
            (
                sds((every, width_d), bf16),
                sds((every, 3 * width), bf16),
                sds((every, width), bf16),
                sds((every, 128), f32),
            ),
            near,
            far,
            wqkv_full,
            qvb_full,
            gs1,
            kmask_row,
            flops=2 * every * width_d * 3 * width + 8 * every * every * 256,
            nbytes=8 << 20,
        )
        kept.append((h1, qkv, att, lse))
    for i in range(images):
        att = kept[i][2]
        attn = scatter_tokens(
            dot(att[:half], wo_full).astype(bf16), dot(att[half:], wo_full).astype(bf16)
        )
        mid = x_own[i].astype(f32) + attn + shift_o
        mids.append(mid)
        h2s.append(gather_tokens(norm_rows(mid, gain2, shift2).astype(bf16)))

    tile = min(256, hidden)
    token = pl.BlockSpec((half, width_d), lambda j: (0, 0))
    outs, mlp = [], []
    for i in range(images):
        parts = call(
            mlp_kernel,
            (
                sds((every, hidden), bf16),
                sds((every, hidden), bf16),
                sds((half, width_d), bf16),
                sds((half, width_d), bf16),
                sds((half, width_d), bf16),
                sds((half, width_d), bf16),
            ),
            *h2s[i],
            *d_all[i],
            w1_full,
            w2_full,
            b1_full,
            flops=8 * every * width_d * hidden,
            nbytes=14 << 20,
            grid=(hidden // tile,),
            in_specs=[
                token,
                token,
                token,
                token,
                pl.BlockSpec((width_d, tile), lambda j: (0, j)),
                pl.BlockSpec((tile, width_d), lambda j: (j, 0)),
                pl.BlockSpec((1, tile), lambda j: (0, j)),
            ],
            out_specs=(
                pl.BlockSpec((every, tile), lambda j: (0, j)),
                pl.BlockSpec((every, tile), lambda j: (0, j)),
                token,
                token,
                token,
                token,
            ),
            scratch_shapes=[pltpu.VMEM((every, width_d), f32), pltpu.VMEM((every, width_d), f32)],
        )
        mlp.append(parts)
    d_mids, sums = [], []
    d_mid_all = []
    for i in range(images):
        d_h2 = scatter_tokens(mlp[i][2], mlp[i][3])
        d_in, d_gain, d_shift = norm_back(mids[i], gain2, d_h2)
        d_mid = d_out[i] + d_in
        d_mids.append(d_mid)
        d_mid_all.append(gather_tokens(d_mid.astype(bf16)))
        sums.append((d_gain, d_shift, jnp.sum(d_mid, axis=0), jnp.sum(d_out[i], axis=0)))
    for i in range(images):
        y = scatter_tokens(mlp[i][4], mlp[i][5])
        outs.append(((mids[i] + y + shift_f) * valid_own).astype(bf16))

    back = []
    for i in range(images):
        h1, qkv, att, lse = kept[i]
        dqkv, dh_keep, dh_send = call(
            attention_back_kernel,
            (
                sds((every, 3 * width), bf16),
                sds((half, width_d), bf16),
                sds((half, width_d), bf16),
            ),
            *d_mid_all[i],
            wo_full,
            wqkv_full,
            qkv,
            att,
            lse,
            kmask_col,
            flops=2 * every * width_d * 4 * width + 20 * every * every * 256,
            nbytes=8 << 20,
            scratch_shapes=[pltpu.VMEM((every, width), bf16)],
        )
        back.append((dqkv, dh_keep, dh_send))
    grad_in = []
    for i in range(images):
        d_h1 = scatter_tokens(back[i][1], back[i][2])
        d_in, d_gain, d_shift = norm_back(x_own[i].astype(f32), gain1, d_h1)
        grad_in.append(d_mids[i] + d_in)
        sums[i] = (d_gain, sums[i][0], d_shift) + sums[i][1:]

    def joined(parts):
        return jnp.concatenate(parts, axis=0)

    h2_all = joined([part for pair in h2s for part in pair])
    d_out_all = joined([part for pair in d_all for part in pair])
    d_mid_cat = joined([part for pair in d_mid_all for part in pair])
    act_all = joined([m[0] for m in mlp])
    dpre_all = joined([m[1] for m in mlp])
    att_all = joined([k[2] for k in kept])
    h1_all = joined([k[0] for k in kept])
    dqkv_all = joined([b[0] for b in back])

    grad_w2 = dot(act_all, d_out_all, TN)
    grad_w1 = dot(h2_all, dpre_all, TN)
    grad_wo = dot(att_all, d_mid_cat, TN)
    grad_wqkv = dot(h1_all, dqkv_all, TN)
    grad_b1 = jnp.sum(dpre_all, axis=0, dtype=f32)
    bias_sums = jnp.sum(dqkv_all, axis=0, dtype=f32).reshape(3, heads, head_dim)
    grad_qvb = jnp.stack([bias_sums[0], bias_sums[2]])
    small_sums = jnp.stack([sum(s[j] for s in sums) for j in range(6)])

    if dp_size == 8:

        def row_block(g):
            count = g.shape[0] // 8
            return lambda k: lax.dynamic_slice_in_dim(g, (dp_index ^ k) * count, count, 0)

        def column_block(g):
            count = g.shape[1] // 8
            return lambda k: lax.dynamic_slice_in_dim(g, (dp_index ^ k) * count, count, 1)

        w2_own = dp_reduce(column_block(grad_w2))
        w1_own = dp_reduce(row_block(grad_w1))
        wo_own = dp_reduce(column_block(grad_wo))
        wqkv_own = dp_reduce(row_block(grad_wqkv))
        pack = jnp.concatenate(
            [
                jnp.transpose(small_sums.reshape(6, 8, -1), (1, 0, 2)),
                jnp.transpose(grad_b1.reshape(-1, 8, b1.shape[1]), (1, 0, 2)).reshape(8, 1, -1),
                jnp.pad(
                    jnp.transpose(
                        grad_qvb.reshape(2 * heads, 8, qv_bias.shape[2]), (1, 0, 2)
                    ).reshape(8, 1, -1),
                    ((0, 0), (0, 0), (0, 128 - qv_bias.size)),
                ),
            ],
            axis=1,
        )
        got = dp_reduce_f32(lambda k: lax.dynamic_index_in_dim(pack, dp_index ^ k, 0, False))
        part = got[:6]
        part = part + hop(part, "tensor", 1)
        part = part + hop(part, "tensor", 2)
        b1_own = got[6].reshape(b1.shape)
        qvb_own = got[7, : qv_bias.size].reshape(qv_bias.shape)
    else:
        scatter = functools.partial(lax.psum_scatter, axis_name="dp", tiled=True)
        w2_own = scatter(grad_w2, scatter_dimension=1)
        w1_own = scatter(grad_w1, scatter_dimension=0)
        wo_own = scatter(grad_wo, scatter_dimension=1)
        wqkv_own = scatter(grad_wqkv, scatter_dimension=0)
        b1_own = scatter(grad_b1.reshape(b1.shape[0], -1), scatter_dimension=1)
        qvb_own = scatter(grad_qvb, scatter_dimension=2)
        part = lax.psum(scatter(small_sums, scatter_dimension=1), "tensor")

    def together(parts):
        return jnp.transpose(jnp.stack(parts)[:, :slots], (1, 0, 2))

    return (
        together(outs),
        together(grad_in),
        wqkv_own.reshape(wqkv.shape),
        qvb_own,
        wo_own,
        w1_own,
        b1_own,
        w2_own,
        part[:2],
        part[2:],
    )


def solution(mesh):
    return jax.shard_map(
        body,
        mesh=mesh,
        in_specs=(
            P("tensor", "dp", None),
            P("dp", None, "tensor"),
            P(None, "tensor", "dp"),
            P("tensor", "dp"),
            P("dp", "tensor"),
            P("tensor", "dp"),
            P("tensor", "dp"),
            P(None, "dp"),
            P(None, "dp"),
            P("tensor", "dp", None),
            P(),
        ),
        out_specs=(
            P("tensor", "dp", None),
            P("tensor", "dp", None),
            P("dp", None, "tensor"),
            P(None, "tensor", "dp"),
            P("tensor", "dp"),
            P("dp", "tensor"),
            P("tensor", "dp"),
            P("tensor", "dp"),
            P(None, "dp"),
            P(None, "dp"),
        ),
        check_vma=False,
    )
```

```python
import functools

import jax
import jax.numpy as jnp
from jax import lax
from jax.experimental import pallas as pl
from jax.experimental.pallas import tpu as pltpu
from jax.sharding import PartitionSpec as P

norm_eps = 1e-06
masked_score = -1e30
f32 = jnp.float32
bf16 = jnp.bfloat16
NT = (((1,), (1,)), ((), ()))
TN = (((0,), (0,)), ((), ()))
NN = (((1,), (0,)), ((), ()))


def dot(a, b, dims=NN):
    return lax.dot_general(a, b, dims, preferred_element_type=f32)


def up(size, step):
    return -(-size // step) * step


def call(kernel, outs, *args, specs=None, chain=None, vmem=40, flops=0, nbytes=0, scalars=0, **kw):
    specs, chain = specs or {}, {k: v for k, v in (chain or {}).items() if v is not None}
    whole = pl.BlockSpec(memory_space=pltpu.VMEM)
    in_specs = [
        specs.get(i, pl.BlockSpec(memory_space=pltpu.SMEM) if i < scalars else whole)
        for i in range(len(args))
    ] + [pl.BlockSpec(memory_space=pl.ANY)] * len(chain)
    count, extra = len(args), len(chain)

    def run(*refs):
        kernel(*refs[:count], *refs[count + extra :])

    return pl.pallas_call(
        run,
        out_shape=tuple(jax.ShapeDtypeStruct(o[0], o[1]) for o in outs),
        in_specs=in_specs,
        out_specs=tuple(o[2] if len(o) > 2 else whole for o in outs),
        input_output_aliases={count + n: k for n, k in enumerate(chain)},
        compiler_params=pltpu.CompilerParams(vmem_limit_bytes=vmem << 20),
        cost_estimate=pl.CostEstimate(flops=flops, bytes_accessed=nbytes, transcendentals=0),
        **kw,
    )(*args, *chain.values())


def hop(x, axis, k):
    size = lax.axis_size(axis)
    return lax.ppermute(x, axis, [(i, i ^ k) for i in range(size)])


def gather_tokens(x, axis=0):
    near = jnp.concatenate([x, hop(x, "tensor", 2)], axis=axis)
    return near, hop(near, "tensor", 1)


def scatter_tokens(keep, send):
    rows = keep.shape[-2] // 2
    total = keep.astype(f32) + hop(send, "tensor", 1).astype(f32)
    return total[..., :rows, :], hop(total[..., rows:, :].astype(bf16), "tensor", 2)


def dp_blocks(x):
    near = {0: x}
    for k in (2, 4, 6):
        near[k] = hop(x, "dp", k)
    blocks = dict(near)
    for k in (0, 2, 4, 6):
        blocks[k + 1] = hop(near[k], "dp", 1)
    return [blocks[k] for k in range(8)]


def dp_reduce(blocks, kind):
    sums = {}
    for k in (6, 4, 2, 0):
        send, keep = blocks[k]
        sums[k] = keep.astype(f32) + hop(send, "dp", 1).astype(f32)
    far = [hop(sums[k].astype(kind), "dp", k).astype(f32) for k in (6, 4, 2)]
    return sums[0] + far[0] + far[1] + far[2]


def spread(at, width):
    t = lax.broadcasted_iota(jnp.int32, (128, width), 1)
    source = lax.broadcasted_iota(jnp.int32, (128, width), 0)
    return ((t // 8) % 8 == at) & (source == (t // 64) * 8 + t % 8)


def place_first(index, *refs):
    *blocks, wqkv, wo, small = refs
    width = wqkv.shape[2]
    rows = wqkv.shape[1] // 8
    total = jnp.zeros((8, small.shape[1]), f32)
    for k, block in enumerate(blocks):
        at = index[0] ^ k
        here = pl.ds(pl.multiple_of(at * 128, 128), 128)
        for c in range(3):
            wqkv[c, here, :] = block[c * rows : (c + 1) * rows, :]
        for a in range(width // 128):
            wo[a * 128 : (a + 1) * 128, here] = block[
                3 * rows + 16 : 4 * rows + 16, a * 128 : (a + 1) * 128
            ]
        part = block[3 * rows : 3 * rows + 16, 0:128][0:8]
        small[0:6, here] = part[0:6].astype(f32)
        total = total + dot(part, spread(at, small.shape[1]).astype(f32).astype(bf16))
    small[6:8, :] = total[6:8]


def pack_small(index, sums, hidden_bias, head_bias, *outs):
    width = sums.shape[1]
    both = jnp.concatenate(
        [
            hidden_bias[...],
            jnp.pad(head_bias[...], ((0, 0), (0, width - head_bias.shape[1]))),
            jnp.zeros((6, width), f32),
        ],
        axis=0,
    )
    for k, out in enumerate(outs):
        at = index[0] ^ k
        here = pl.ds(pl.multiple_of(at * 128, 128), 128)
        out[0:6, :] = sums[0:6, here]
        out[6:8, :] = lax.dot_general(
            both,
            spread(at, width).astype(f32),
            NT,
            precision=lax.Precision.HIGHEST,
            preferred_element_type=f32,
        )[0:2]


def pack_last(index, g_qkv, g_o, *outs):
    for n, k in enumerate((6, 4, 2, 0)):
        for m, out in ((k + 1, outs[2 * n]), (k, outs[2 * n + 1])):
            at = index[0] ^ m
            here = pl.ds(pl.multiple_of(at * 128, 128), 128)
            out[:, 0 : g_qkv.shape[1]] = g_qkv[here, :].astype(out.dtype)
            for a in range(g_o.shape[0] // 128):
                lo = g_qkv.shape[1] + a * 128
                out[:, lo : lo + 128] = g_o[a * 128 : (a + 1) * 128, here].astype(out.dtype)


def norm_rows(x, gain, shift):
    mean = jnp.mean(x, axis=-1, keepdims=True)
    centered = x - mean
    var = jnp.mean(centered * centered, axis=-1, keepdims=True)
    return centered * lax.rsqrt(var + norm_eps) * gain + shift


def attention_kernel(near, far, wqkv, small, kmask, h1, qkv, att, lse):
    half = near.shape[0]
    rows = 2 * half
    width = wqkv.shape[2]
    for i, ref in enumerate((near, far)):
        x = ref[...].astype(f32)
        h1[i * half : (i + 1) * half, :] = norm_rows(x, small[0:1, :], small[2:3, :]).astype(bf16)
    for c in range(3):
        out = dot(h1[...], wqkv[c])
        if c != 1:
            out = out + small[7:8, (c // 2) * width : (c // 2 + 1) * width]
        out = out.astype(bf16)
        if c == 0:
            out = out * bf16(0.125)
        qkv[:, c * width : (c + 1) * width] = out
    lane = lax.broadcasted_iota(jnp.int32, (1, 128), 1)
    lane_f = lane
    lse_parts = [jnp.zeros((half, 128), f32) for _ in range(2)]
    for p in range(width // 128):
        keys = qkv[:, width + p * 128 : width + (p + 1) * 128]
        vals = qkv[:, 2 * width + p * 128 : 2 * width + (p + 1) * 128]
        outs = [jnp.zeros((half, 128), f32) for _ in range(2)]
        for h in range(2):
            mine = (lane >= 64 * h) & (lane < 64 * h + 64)
            k_h = jnp.where(mine, keys, bf16(0))
            v_h = jnp.where(mine, vals, bf16(0))
            for b in range(2):
                q = qkv[b * half : (b + 1) * half, p * 128 : (p + 1) * 128]
                s = dot(q, k_h, NT) + kmask[...]
                top = jnp.max(s, axis=-1, keepdims=True)
                e = jnp.exp(s - top)
                total = jnp.sum(e, axis=-1, keepdims=True)
                outs[b] = outs[b] + dot(e.astype(bf16), v_h) / total
                lse_parts[b] = jnp.where(
                    lane_f == 2 * p + h, top + jnp.log(total), lse_parts[b]
                )
        for b in range(2):
            att[b * half : (b + 1) * half, p * 128 : (p + 1) * 128] = outs[b].astype(bf16)
    for b in range(2):
        lse[b * half : (b + 1) * half, :] = lse_parts[b]


def attention_back_kernel(
    near, far, wo, wqkv, qkv, att, lse, kmask, dqkv, d_mid, dh_keep, dh_send, d_att
):
    half = near.shape[0]
    rows = 2 * half
    width = wo.shape[0]
    for i, ref in enumerate((near, far)):
        d_mid[i * half : (i + 1) * half, :] = ref[...]
        d_att[i * half : (i + 1) * half, :] = dot(ref[...], wo[...], NT).astype(bf16)
    prod = d_att[...].astype(f32) * att[...].astype(f32)
    heads = width // 64
    pick_d = (
        lax.broadcasted_iota(jnp.int32, (8, width), 1) // 64
        == lax.broadcasted_iota(jnp.int32, (8, width), 0)
    ).astype(f32)
    pick_l = (
        lax.broadcasted_iota(jnp.int32, (8, 128), 1)
        == lax.broadcasted_iota(jnp.int32, (8, 128), 0)
    ).astype(f32)
    row_dot = lax.dot_general(
        pick_d, prod, NT, precision=lax.Precision.HIGHEST, preferred_element_type=f32
    )
    row_lse = lax.dot_general(
        pick_l, lse[...], NT, precision=lax.Precision.HIGHEST, preferred_element_type=f32
    )
    lane = lax.broadcasted_iota(jnp.int32, (1, 128), 1)
    for p in range(width // 128):
        cols = slice(p * 128, (p + 1) * 128)
        q = qkv[:, p * 128 : (p + 1) * 128]
        d_o = d_att[:, cols]
        dq = jnp.zeros((rows, 128), f32)
        for b in range(2):
            block = slice(b * half, (b + 1) * half)
            keys = qkv[block, width + p * 128 : width + (p + 1) * 128]
            vals = qkv[block, 2 * width + p * 128 : 2 * width + (p + 1) * 128]
            dk = jnp.zeros((half, 128), f32)
            dv = jnp.zeros((half, 128), f32)
            for h in range(2):
                mine = (lane >= 64 * h) & (lane < 64 * h + 64)
                k_h = jnp.where(mine, keys, bf16(0))
                v_h = jnp.where(mine, vals, bf16(0))
                at = 2 * p + h
                s = dot(k_h, q, NT) + kmask[block, :]
                probs = jnp.exp(s - row_lse[at : at + 1, :])
                d_p = dot(v_h, d_o, NT)
                d_s = (probs * (d_p - row_dot[at : at + 1, :])).astype(bf16)
                dv = dv + dot(probs.astype(bf16), jnp.where(mine, d_o, bf16(0)))
                dk = dk + dot(d_s, jnp.where(mine, q, bf16(0)))
                dq = dq + dot(d_s, k_h, TN)
            dqkv[block, width + p * 128 : width + (p + 1) * 128] = dk.astype(bf16)
            dqkv[block, 2 * width + p * 128 : 2 * width + (p + 1) * 128] = dv.astype(bf16)
        dqkv[:, p * 128 : (p + 1) * 128] = (dq * 0.125).astype(bf16)
    for i, ref in enumerate((dh_keep, dh_send)):
        block = slice(i * half, (i + 1) * half)
        total = dot(dqkv[block, 0:width], wqkv[0], NT)
        for c in (1, 2):
            total = total + dot(dqkv[block, c * width : (c + 1) * width], wqkv[c], NT)
        ref[...] = total.astype(bf16)


def gelu_parts(u):
    e = jnp.exp(-0.5 * u * u)
    t = 1.0 / (1.0 + (0.3275911 * 0.7071067811865476) * jnp.abs(u))
    poly = t * (
        0.5 * 0.254829592
        + t
        * (
            0.5 * -0.284496736
            + t * (0.5 * 1.421413741 + t * (0.5 * -1.453152027 + t * (0.5 * 1.061405429)))
        )
    )
    tail = poly * e
    phi_sum = jnp.where(u >= 0, 1.0 - tail, tail)
    return u * phi_sum, phi_sum + u * (e * 0.3989422804014327)


def mlp_kernel(
    near,
    far,
    dnear,
    dfar,
    w1,
    w2,
    small,
    act,
    dpre,
    h2,
    d_out,
    dh_keep,
    dh_send,
    y_keep,
    y_send,
    acc_d,
    acc_y,
):
    step = pl.program_id(0)
    half = near.shape[0]
    depth, tile = near.shape[1], act.shape[1]

    @pl.when(step == 0)
    def _():
        acc_d[...] = jnp.zeros_like(acc_d)
        acc_y[...] = jnp.zeros_like(acc_y)
        for i, (h_ref, d_ref) in enumerate(((near, dnear), (far, dfar))):
            h2[i * half : (i + 1) * half, :] = h_ref[...]
            d_out[i * half : (i + 1) * half, :] = d_ref[...]

    w1_tile = w1[...].reshape(depth, tile)
    w2_tile = jnp.concatenate(
        [
            jnp.concatenate(
                [w2[d, :, a * 128 : (a + 1) * 128] for d in range(w2.shape[0])], axis=1
            )
            for a in range(tile // 128)
        ],
        axis=0,
    )
    bias = small[6:7, pl.ds(pl.multiple_of(step * tile, 128), tile)]
    for i, (h_ref, d_ref) in enumerate(((near, dnear), (far, dfar))):
        block = slice(i * half, (i + 1) * half)
        pre = dot(h_ref[...], w1_tile) + bias
        d_act = dot(d_ref[...], w2_tile, NT)
        value, slope = gelu_parts(pre)
        value = value.astype(bf16)
        grad = (d_act * slope).astype(bf16)
        act[block, :] = value
        dpre[block, :] = grad
        acc_d[block, :] += dot(grad, w1_tile, NT)
        acc_y[block, :] += dot(value, w2_tile)

    @pl.when(step == pl.num_programs(0) - 1)
    def _():
        dh_keep[...] = acc_d[0:half, :].astype(bf16)
        dh_send[...] = acc_d[half:, :].astype(bf16)
        y_keep[...] = acc_y[0:half, :].astype(bf16)
        y_send[...] = acc_y[half:, :].astype(bf16)


def norm_kernel(own, far, x, small, mid, h2):
    total = x[...].astype(f32) + own[...] + far[...].astype(f32) + small[4:5, :]
    mid[...] = total
    h2[...] = norm_rows(total, small[1:2, :], small[3:4, :]).astype(bf16)


def norm_back_rows(values, gain, grad):
    mean = jnp.mean(values, axis=-1, keepdims=True)
    centered = values - mean
    var = jnp.mean(centered * centered, axis=-1, keepdims=True)
    r = lax.rsqrt(var + norm_eps)
    xhat = centered * r
    f = grad * gain
    d_in = r * (
        f
        - jnp.mean(f, axis=-1, keepdims=True)
        - xhat * jnp.mean(f * xhat, axis=-1, keepdims=True)
    )
    return d_in, jnp.sum(grad * xhat, axis=0, keepdims=True), jnp.sum(grad, axis=0, keepdims=True)


def norm_back_kernel(row, own, far, values, beside, small, wide, *rest):
    sums = rest[-1]
    d_in, d_gain, d_shift = norm_back_rows(
        values[...].astype(f32), small[row : row + 1, :], own[...] + far[...].astype(f32)
    )
    total = beside[...].astype(f32) + d_in
    wide[...] = total
    parts = [d_gain, d_shift]
    if len(rest) > 1:
        rest[0][...] = total.astype(bf16)
        parts += [
            jnp.sum(total, axis=0, keepdims=True),
            jnp.sum(beside[...].astype(f32), axis=0, keepdims=True),
        ]
    parts.append(jnp.zeros((8 - len(parts), d_in.shape[1]), f32))
    sums[...] = jnp.concatenate(parts, axis=0)


def body(inputs, wqkv, qv_bias, wo, w1, b1, w2, gains, shifts, cotangent, span_lengths):
    slots, images, width_d = inputs.shape
    dp_size = lax.axis_size("dp")
    dp_index = lax.axis_index("dp")
    rank = lax.axis_index("tensor")
    rows = up(slots, 8)
    half, every = 2 * rows, 4 * rows
    total_rows = images * every
    width = wqkv.shape[2]
    heads, head_dim = qv_bias.shape[1], qv_bias.shape[2] * dp_size
    hidden = w1.shape[1]

    def apart(x):
        return jnp.pad(jnp.transpose(x, (1, 0, 2)), ((0, 0), (0, rows - slots), (0, 0)))

    x_own = apart(inputs)
    slot = jnp.arange(rows, dtype=jnp.int32)

    def used(k):
        return slot < lax.dynamic_index_in_dim(span_lengths, rank ^ k, keepdims=False)

    valid_own = used(0).astype(f32)[:, None]
    kmask = jnp.where(
        jnp.concatenate([used(0), used(2), used(1), used(3)]), 0.0, masked_score
    ).astype(f32)
    kmask_row, kmask_col = kmask[None, :], kmask[:, None]

    x_all = [gather_tokens(x_own[i]) for i in range(images)]

    index = dp_index.astype(jnp.int32)[None]
    if dp_size == 8:
        late = jnp.stack(
            [
                w1,
                jnp.transpose(w2.reshape(hidden // 128, 128, 128), (1, 0, 2)).reshape(128, hidden),
            ]
        )
        late = lax.all_gather(late, "dp", axis=1, tiled=False)
        w1_full, w2_full = late[0], late[1]
        small = jnp.concatenate(
            [
                gains,
                shifts,
                b1.reshape(1, -1),
                jnp.pad(qv_bias.reshape(1, -1), ((0, 0), (0, 128 - qv_bias.size))),
            ]
        )
        first = jnp.concatenate(
            [
                jnp.transpose(wqkv, (1, 0, 2)).reshape(-1, width),
                jnp.pad(small, ((0, 8), (0, width - 128))),
                jnp.transpose(wo.reshape(width // 128, 128, 128), (1, 0, 2)).reshape(128, width),
            ]
        )
        wqkv_full, wo_full, small_full = call(
            place_first,
            (((3, width_d, width), bf16), ((width, width_d), bf16), ((8, width_d), f32)),
            index,
            *dp_blocks(first),
            scalars=1,
            nbytes=4 << 20,
        )
    else:
        wqkv_full = jnp.transpose(lax.all_gather(wqkv, "dp", axis=0, tiled=True), (1, 0, 2))
        wo_full = lax.all_gather(wo, "dp", axis=1, tiled=True)
        w1_full = lax.all_gather(w1, "dp", axis=0, tiled=True).reshape(8, -1, hidden)
        w2_full = lax.all_gather(w2, "dp", axis=1, tiled=True)
        w2_full = jnp.transpose(
            w2_full.reshape(hidden // 128, 128, width_d // 128, 128), (2, 1, 0, 3)
        ).reshape(width_d // 128, 128, hidden)
        qvb = lax.all_gather(qv_bias, "dp", axis=2, tiled=True).reshape(1, -1)
        small_full = jnp.concatenate(
            [
                lax.all_gather(jnp.concatenate([gains, shifts]), "dp", axis=1, tiled=True),
                lax.all_gather(b1, "dp", axis=1, tiled=True).reshape(1, hidden),
                jnp.pad(qvb, ((0, 0), (0, width_d - qvb.size))),
            ]
        ).astype(f32)

    d_out = (apart(cotangent).astype(f32) * valid_own).astype(bf16)
    d_near, d_far = gather_tokens(d_out, axis=1)

    def block_of(i, n):
        return pl.BlockSpec((every, n), lambda *_: (i, 0))

    def image_of(i, n):
        return pl.BlockSpec((None, n, width_d), lambda *_: (i, 0, 0))

    h1_all = att_all = None
    kept, mids, h2s = [], [], []
    for i in range(images):
        h1_all, qkv, att_all, lse = call(
            attention_kernel,
            (
                ((total_rows, width_d), bf16, block_of(i, width_d)),
                ((every, 3 * width), bf16),
                ((total_rows, width), bf16, block_of(i, width)),
                ((every, 128), f32),
            ),
            *x_all[i],
            wqkv_full,
            small_full,
            kmask_row,
            chain={0: h1_all, 2: att_all},
            grid=(1,),
            flops=2 * every * width_d * 3 * width + 8 * every * every * 256,
            nbytes=8 << 20,
        )
        kept.append((qkv, lse))
        att = lax.dynamic_slice_in_dim(att_all, i * every, every, 0)
        own, far = scatter_tokens(
            dot(att[:half], wo_full).astype(bf16), dot(att[half:], wo_full).astype(bf16)
        )
        mid, h2 = call(
            norm_kernel,
            (((rows, width_d), f32), ((rows, width_d), bf16)),
            own,
            far,
            x_own[i],
            small_full,
            nbytes=2 << 20,
        )
        mids.append(mid)
        h2s.append(gather_tokens(h2))

    tile = min(512, hidden)
    token = pl.BlockSpec((half, width_d), lambda j: (0, 0))
    act_all = dpre_all = h2_all = d_out_all = y_keep = y_send = None
    d_mids, d_mid_all, sums = [], [], []
    for i in range(images):
        act_all, dpre_all, h2_all, d_out_all, dh_keep, dh_send, y_keep, y_send = call(
            mlp_kernel,
            (
                ((total_rows, hidden), bf16, pl.BlockSpec((every, tile), lambda j, i=i: (i, j))),
                ((total_rows, hidden), bf16, pl.BlockSpec((every, tile), lambda j, i=i: (i, j))),
                ((total_rows, width_d), bf16, block_of(i, width_d)),
                ((total_rows, width_d), bf16, block_of(i, width_d)),
                ((half, width_d), bf16, token),
                ((half, width_d), bf16, token),
                ((images, half, width_d), bf16, image_of(i, half)),
                ((images, half, width_d), bf16, image_of(i, half)),
            ),
            *h2s[i],
            d_near,
            d_far,
            w1_full,
            w2_full,
            small_full,
            specs={
                0: token,
                1: token,
                2: image_of(i, half),
                3: image_of(i, half),
                4: pl.BlockSpec((8, width_d // 8, tile), lambda j: (0, 0, j)),
                5: pl.BlockSpec((width_d // 128, 128, tile), lambda j: (0, 0, j)),
                6: pl.BlockSpec((8, width_d), lambda j: (0, 0)),
            },
            chain={
                0: act_all,
                1: dpre_all,
                2: h2_all,
                3: d_out_all,
                6: y_keep,
                7: y_send,
            },
            vmem=48,
            flops=8 * every * width_d * hidden,
            nbytes=14 << 20,
            grid=(hidden // tile,),
            scratch_shapes=[pltpu.VMEM((every, width_d), f32), pltpu.VMEM((every, width_d), f32)],
        )
        own, far = scatter_tokens(dh_keep, dh_send)
        d_mid, d_mid_b, part = call(
            functools.partial(norm_back_kernel, 1),
            (((rows, width_d), f32), ((rows, width_d), bf16), ((8, width_d), f32)),
            own,
            far,
            mids[i],
            d_out[i],
            small_full,
            nbytes=3 << 20,
        )
        d_mids.append(d_mid)
        sums.append(part)
        d_mid_all.append(gather_tokens(d_mid_b))

    grad_w2 = dot(act_all, d_out_all, TN)
    grad_w1 = dot(h2_all, dpre_all, TN)
    grad_b1 = jnp.sum(dpre_all, axis=0, dtype=f32)
    if dp_size == 8:
        late = jnp.stack(
            [
                grad_w1.astype(bf16).reshape(8, 128, hidden),
                jnp.transpose(
                    grad_w2.astype(bf16).reshape(hidden // 128, 128, 8, 128), (2, 1, 0, 3)
                ).reshape(8, 128, hidden),
            ],
            axis=1,
        ).reshape(8 * 256, hidden)
        late = lax.psum_scatter(late, "dp", scatter_dimension=0, tiled=True).astype(f32)
        w1_own = late[:128]
        w2_own = jnp.transpose(late[128:].reshape(128, hidden // 128, 128), (1, 0, 2)).reshape(
            w2.shape
        )

    own, far = scatter_tokens(y_keep, y_send)
    outs = jnp.stack(mids) + own + far.astype(f32) + small_full[5]
    outs = (outs * valid_own).astype(bf16)

    dqkv_all = d_mid_cat = None
    grad_in, sums1 = [], []
    for i in range(images):
        qkv, lse = kept[i]
        dqkv_all, d_mid_cat, dh_keep, dh_send = call(
            attention_back_kernel,
            (
                ((total_rows, 3 * width), bf16, block_of(i, 3 * width)),
                ((total_rows, width_d), bf16, block_of(i, width_d)),
                ((half, width_d), bf16),
                ((half, width_d), bf16),
            ),
            *d_mid_all[i],
            wo_full,
            wqkv_full,
            qkv,
            att_all,
            lse,
            kmask_col,
            specs={5: block_of(i, width)},
            chain={0: dqkv_all, 1: d_mid_cat},
            grid=(1,),
            flops=2 * every * width_d * 4 * width + 20 * every * every * 256,
            nbytes=8 << 20,
            scratch_shapes=[pltpu.VMEM((every, width), bf16)],
        )
        own, far = scatter_tokens(dh_keep, dh_send)
        d_in, part = call(
            functools.partial(norm_back_kernel, 0),
            (((rows, width_d), f32), ((8, width_d), f32)),
            own,
            far,
            x_own[i],
            d_mids[i],
            small_full,
            nbytes=3 << 20,
        )
        grad_in.append(d_in)
        sums1.append(part)

    grad_wo = dot(att_all, d_mid_cat, TN)
    grad_wqkv = dot(h1_all, dqkv_all, TN)
    bias_sums = jnp.sum(dqkv_all, axis=0, dtype=f32)
    head_bias = jnp.concatenate([bias_sums[:width], bias_sums[2 * width :]])
    sum1, sum2 = sum(sums1), sum(sums)
    small_sums = jnp.stack(
        [sum1[0], sum2[0], sum1[1], sum2[1], sum2[2], sum2[3], sum2[7], sum2[7]]
    )
    if dp_size == 8:
        block = (128, 3 * width + width)
        last = call(
            pack_last,
            ((block, bf16), (block, f32)) * 4,
            index,
            grad_wqkv,
            grad_wo,
            scalars=1,
            nbytes=8 << 20,
        )
        own = dp_reduce({k: last[2 * n : 2 * n + 2] for n, k in enumerate((6, 4, 2, 0))}, bf16)
        wqkv_own = jnp.transpose(own[:, : 3 * width].reshape(128, 3, width), (0, 1, 2))
        wo_own = jnp.transpose(
            own[:, 3 * width :].reshape(128, width // 128, 128), (1, 0, 2)
        ).reshape(wo.shape)
        tiny = call(
            pack_small,
            (((8, 128), f32),) * 8,
            index,
            small_sums,
            grad_b1[None, :],
            head_bias[None, :],
            scalars=1,
        )
        got = dp_reduce({k: (tiny[k + 1], tiny[k]) for k in (6, 4, 2, 0)}, f32)
        part = got[:6]
        part = part + hop(part, "tensor", 1)
        part = part + hop(part, "tensor", 2)
        b1_own = got[6].reshape(b1.shape)
        qvb_own = got[7, : qv_bias.size].reshape(qv_bias.shape)
    else:
        scatter = functools.partial(lax.psum_scatter, axis_name="dp", tiled=True)
        w2_own = scatter(grad_w2, scatter_dimension=1)
        w1_own = scatter(grad_w1, scatter_dimension=0)
        wo_own = scatter(grad_wo, scatter_dimension=1)
        wqkv_own = scatter(grad_wqkv, scatter_dimension=0).reshape(wqkv.shape)
        b1_own = scatter(grad_b1.reshape(b1.shape[0], -1), scatter_dimension=1)
        qvb_own = scatter(head_bias.reshape(2, heads, head_dim), scatter_dimension=2)
        part = lax.psum(scatter(small_sums[:6], scatter_dimension=1), "tensor")

    def together(parts):
        return jnp.transpose(parts[:, :slots], (1, 0, 2))

    return (
        together(outs),
        together(jnp.stack(grad_in)),
        wqkv_own.reshape(wqkv.shape),
        qvb_own,
        wo_own,
        w1_own,
        b1_own,
        w2_own,
        part[:2],
        part[2:],
    )


def solution(mesh):
    return jax.shard_map(
        body,
        mesh=mesh,
        in_specs=(
            P("tensor", "dp", None),
            P("dp", None, "tensor"),
            P(None, "tensor", "dp"),
            P("tensor", "dp"),
            P("dp", "tensor"),
            P("tensor", "dp"),
            P("tensor", "dp"),
            P(None, "dp"),
            P(None, "dp"),
            P("tensor", "dp", None),
            P(),
        ),
        out_specs=(
            P("tensor", "dp", None),
            P("tensor", "dp", None),
            P("dp", None, "tensor"),
            P(None, "tensor", "dp"),
            P("tensor", "dp"),
            P("dp", "tensor"),
            P("tensor", "dp"),
            P("tensor", "dp"),
            P(None, "dp"),
            P(None, "dp"),
        ),
        check_vma=False,
    )
```

```python
import functools

import jax
import jax.numpy as jnp
from jax import lax
from jax.experimental import pallas as pl
from jax.experimental.pallas import tpu as pltpu
from jax.sharding import PartitionSpec as P

norm_eps = 1e-06
masked_score = -1e30
f32 = jnp.float32
bf16 = jnp.bfloat16
NT = (((1,), (1,)), ((), ()))
TN = (((0,), (0,)), ((), ()))
NN = (((1,), (0,)), ((), ()))


def dot(a, b, dims=NN):
    return lax.dot_general(a, b, dims, preferred_element_type=f32)


def up(size, step):
    return -(-size // step) * step


cost_part = 64


def call(kernel, outs, *args, specs=None, chain=None, vmem=40, flops=0, nbytes=0, scalars=0, **kw):
    specs, chain = specs or {}, {k: v for k, v in (chain or {}).items() if v is not None}
    whole = pl.BlockSpec(memory_space=pltpu.VMEM)

    def spec(i, x):
        if i < scalars:
            return pl.BlockSpec(memory_space=pltpu.SMEM)
        if i in specs or "grid" not in kw:
            return specs.get(i, whole)
        return pl.BlockSpec(x.shape, lambda *_: (0,) * x.ndim)

    in_specs = [spec(i, x) for i, x in enumerate(args)] + [pl.BlockSpec(memory_space=pl.ANY)] * len(chain)
    count, extra = len(args), len(chain)

    def run(*refs):
        kernel(*refs[:count], *refs[count + extra :])

    return pl.pallas_call(
        run,
        out_shape=tuple(jax.ShapeDtypeStruct(o[0], o[1]) for o in outs),
        in_specs=in_specs,
        out_specs=tuple(o[2] if len(o) > 2 else whole for o in outs),
        input_output_aliases={count + n: k for n, k in enumerate(chain)},
        compiler_params=pltpu.CompilerParams(vmem_limit_bytes=vmem << 20),
        cost_estimate=pl.CostEstimate(
            flops=flops // cost_part, bytes_accessed=nbytes // cost_part, transcendentals=0
        ),
        **kw,
    )(*args, *chain.values())


def after(x, *deps):
    return lax.optimization_barrier((x, *deps))[0]


def hop(x, axis, k):
    size = lax.axis_size(axis)
    return lax.ppermute(x, axis, [(i, i ^ k) for i in range(size)])


def gather_core(x, far, axis=0):
    near = jnp.concatenate([x, far], axis=axis)
    return near, hop(near, "tensor", 1)


def gather_tokens(x):
    return gather_core(x, hop(x, "tensor", 2))


def scatter_core(keep, send):
    rows = keep.shape[-2] // 2
    got = hop(send, "tensor", 1)
    own = keep[..., :rows, :].astype(f32) + got[..., :rows, :].astype(f32)
    far = keep[..., rows:, :].astype(f32) + got[..., rows:, :].astype(f32)
    return own, far.astype(bf16)


def dp_blocks_begin(x):
    return [hop(x, "dp", k) for k in (1, 2, 4, 6)]


def dp_blocks_end(x, got):
    side, *far = got
    near = [x, *far]
    other = [side, *(hop(b, "dp", 1) for b in far)]
    return [b for pair in zip(near, other, strict=True) for b in pair]


def dp_reduce_begin(send_far, send_near, keep_far, keep_near, far, *deps):
    if deps:
        far = after(far, *deps)
    near = hop(after(send_near, far), "dp", 1).astype(f32)
    far = keep_far.astype(f32) + far.astype(f32)
    near = keep_near.astype(f32) + near
    return {6: far[0], 4: far[1], 2: near[0], 0: near[1]}


def dp_reduce_far(sums, kind, offsets):
    return [hop(sums[k].astype(kind), "dp", k).astype(f32) for k in offsets]


def spread(at, width):
    t = lax.broadcasted_iota(jnp.int32, (128, width), 1)
    source = lax.broadcasted_iota(jnp.int32, (128, width), 0)
    return ((t // 8) % 8 == at) & (source == (t // 64) * 8 + t % 8)


def place_first(index, *refs):
    *blocks, wqkv, wo, small = refs
    width = wqkv.shape[2]
    rows = wqkv.shape[1] // 8
    total = jnp.zeros((8, small.shape[1]), f32)
    for k, block in enumerate(blocks):
        at = index[0] ^ k
        here = pl.ds(pl.multiple_of(at * 128, 128), 128)
        for c in range(3):
            wqkv[c, here, :] = block[c * rows : (c + 1) * rows, :]
        for a in range(width // 128):
            wo[a * 128 : (a + 1) * 128, here] = block[
                3 * rows + 16 : 4 * rows + 16, a * 128 : (a + 1) * 128
            ]
        part = block[3 * rows : 3 * rows + 16, 0:128][0:8]
        small[0:6, here] = part[0:6].astype(f32)
        total = total + dot(part, spread(at, small.shape[1]).astype(f32).astype(bf16))
    small[6:8, :] = total[6:8]


def pack_small(index, sums, hidden_bias, head_bias, send, keep):
    width = sums.shape[1]
    both = jnp.concatenate(
        [
            hidden_bias[...],
            jnp.pad(head_bias[...], ((0, 0), (0, width - head_bias.shape[1]))),
            jnp.zeros((6, width), f32),
        ],
        axis=0,
    )
    for k in range(8):
        at = index[0] ^ k
        out = (keep, send)[k % 2].at[k // 2]
        here = pl.ds(pl.multiple_of(at * 128, 128), 128)
        out[0:6, :] = sums[0:6, here]
        out[6:8, :] = lax.dot_general(
            both,
            spread(at, width).astype(f32),
            NT,
            precision=lax.Precision.HIGHEST,
            preferred_element_type=f32,
        )[0:2]


def pack_columns(index, grad, *outs):
    for n, k in enumerate((6, 4, 2, 0)):
        for m, out in ((k + 1, outs[n // 2].at[n % 2]), (k, outs[2 + n // 2].at[n % 2])):
            at = index[0] ^ m
            out[...] = grad[:, pl.ds(pl.multiple_of(at * 128, 128), 128)]


def pack_last(index, g_qkv, g_o, *outs):
    for n, k in enumerate((6, 4, 2, 0)):
        for m, out in ((k + 1, outs[n // 2].at[n % 2]), (k, outs[2 + n // 2].at[n % 2])):
            at = index[0] ^ m
            here = pl.ds(pl.multiple_of(at * 128, 128), 128)
            out[:, 0 : g_qkv.shape[1]] = g_qkv[here, :].astype(out.dtype)
            for a in range(g_o.shape[0] // 128):
                lo = g_qkv.shape[1] + a * 128
                out[:, lo : lo + 128] = g_o[a * 128 : (a + 1) * 128, here].astype(out.dtype)


def norm_rows(x, gain, shift):
    mean = jnp.mean(x, axis=-1, keepdims=True)
    centered = x - mean
    var = jnp.mean(centered * centered, axis=-1, keepdims=True)
    return centered * lax.rsqrt(var + norm_eps) * gain + shift


def attention_kernel(near, far, wqkv, small, kmask, h1, qkv, att, lse):
    half = near.shape[0]
    rows = 2 * half
    width = wqkv.shape[2]
    for i, ref in enumerate((near, far)):
        x = ref[...].astype(f32)
        h1[i * half : (i + 1) * half, :] = norm_rows(x, small[0:1, :], small[2:3, :]).astype(bf16)
    for c in range(3):
        out = dot(h1[...], wqkv[c])
        if c != 1:
            out = out + small[7:8, (c // 2) * width : (c // 2 + 1) * width]
        out = out.astype(bf16)
        if c == 0:
            out = out * bf16(0.125)
        qkv[:, c * width : (c + 1) * width] = out
    lane = lax.broadcasted_iota(jnp.int32, (1, 128), 1)
    lane_f = lane
    lse_parts = [jnp.zeros((half, 128), f32) for _ in range(2)]
    for p in range(width // 128):
        keys = qkv[:, width + p * 128 : width + (p + 1) * 128]
        vals = qkv[:, 2 * width + p * 128 : 2 * width + (p + 1) * 128]
        outs = [jnp.zeros((half, 128), f32) for _ in range(2)]
        for h in range(2):
            mine = (lane >= 64 * h) & (lane < 64 * h + 64)
            k_h = jnp.where(mine, keys, bf16(0))
            v_h = jnp.where(mine, vals, bf16(0))
            for b in range(2):
                q = qkv[b * half : (b + 1) * half, p * 128 : (p + 1) * 128]
                s = dot(q, k_h, NT) + kmask[...]
                top = jnp.max(s, axis=-1, keepdims=True)
                e = jnp.exp(s - top)
                total = jnp.sum(e, axis=-1, keepdims=True)
                outs[b] = outs[b] + dot(e.astype(bf16), v_h) / total
                lse_parts[b] = jnp.where(
                    lane_f == 2 * p + h, top + jnp.log(total), lse_parts[b]
                )
        for b in range(2):
            att[b * half : (b + 1) * half, p * 128 : (p + 1) * 128] = outs[b].astype(bf16)
    for b in range(2):
        lse[b * half : (b + 1) * half, :] = lse_parts[b]


def attention_back_kernel(
    near, far, wo, wqkv, qkv, att, lse, kmask, dqkv, d_mid, bias_sum, dh_keep, dh_send, d_att
):
    half = near.shape[0]
    rows = 2 * half
    width = wo.shape[0]
    for i, ref in enumerate((near, far)):
        d_mid[i * half : (i + 1) * half, :] = ref[...]
        d_att[i * half : (i + 1) * half, :] = dot(ref[...], wo[...], NT).astype(bf16)
    prod = d_att[...].astype(f32) * att[...].astype(f32)
    heads = width // 64
    pick_d = (
        lax.broadcasted_iota(jnp.int32, (8, width), 1) // 64
        == lax.broadcasted_iota(jnp.int32, (8, width), 0)
    ).astype(f32)
    pick_l = (
        lax.broadcasted_iota(jnp.int32, (8, 128), 1)
        == lax.broadcasted_iota(jnp.int32, (8, 128), 0)
    ).astype(f32)
    row_dot = lax.dot_general(
        pick_d, prod, NT, precision=lax.Precision.HIGHEST, preferred_element_type=f32
    )
    row_lse = lax.dot_general(
        pick_l, lse[...], NT, precision=lax.Precision.HIGHEST, preferred_element_type=f32
    )
    lane = lax.broadcasted_iota(jnp.int32, (1, 128), 1)
    for p in range(width // 128):
        cols = slice(p * 128, (p + 1) * 128)
        q = qkv[:, p * 128 : (p + 1) * 128]
        d_o = d_att[:, cols]
        dq = jnp.zeros((rows, 128), f32)
        for b in range(2):
            block = slice(b * half, (b + 1) * half)
            keys = qkv[block, width + p * 128 : width + (p + 1) * 128]
            vals = qkv[block, 2 * width + p * 128 : 2 * width + (p + 1) * 128]
            dk = jnp.zeros((half, 128), f32)
            dv = jnp.zeros((half, 128), f32)
            for h in range(2):
                mine = (lane >= 64 * h) & (lane < 64 * h + 64)
                k_h = jnp.where(mine, keys, bf16(0))
                v_h = jnp.where(mine, vals, bf16(0))
                at = 2 * p + h
                s = dot(k_h, q, NT) + kmask[block, :]
                probs = jnp.exp(s - row_lse[at : at + 1, :])
                d_p = dot(v_h, d_o, NT)
                d_s = (probs * (d_p - row_dot[at : at + 1, :])).astype(bf16)
                dv = dv + dot(probs.astype(bf16), jnp.where(mine, d_o, bf16(0)))
                dk = dk + dot(d_s, jnp.where(mine, q, bf16(0)))
                dq = dq + dot(d_s, k_h, TN)
            dqkv[block, width + p * 128 : width + (p + 1) * 128] = dk.astype(bf16)
            dqkv[block, 2 * width + p * 128 : 2 * width + (p + 1) * 128] = dv.astype(bf16)
        dqkv[:, p * 128 : (p + 1) * 128] = (dq * 0.125).astype(bf16)
    bias_sum[...] = jnp.broadcast_to(
        jnp.sum(dqkv[...].astype(f32), axis=0, keepdims=True), bias_sum.shape
    )
    for i, ref in enumerate((dh_keep, dh_send)):
        block = slice(i * half, (i + 1) * half)
        total = dot(dqkv[block, 0:width], wqkv[0], NT)
        for c in (1, 2):
            total = total + dot(dqkv[block, c * width : (c + 1) * width], wqkv[c], NT)
        ref[...] = total.astype(bf16)


def gelu_parts(u):
    e = jnp.exp(-0.5 * u * u)
    t = 1.0 / (1.0 + (0.3275911 * 0.7071067811865476) * jnp.abs(u))
    poly = t * (
        0.5 * 0.254829592
        + t
        * (
            0.5 * -0.284496736
            + t * (0.5 * 1.421413741 + t * (0.5 * -1.453152027 + t * (0.5 * 1.061405429)))
        )
    )
    tail = poly * e
    phi_sum = jnp.where(u >= 0, 1.0 - tail, tail)
    return u * phi_sum, phi_sum + u * (e * 0.3989422804014327)


def mlp_kernel(
    near,
    far,
    dnear,
    dfar,
    w1,
    w2,
    small,
    act,
    dpre,
    h2,
    d_out,
    bias_sum,
    dh_keep,
    dh_send,
    y_keep,
    y_send,
    acc_d,
    acc_y,
):
    step = pl.program_id(0)
    half = near.shape[0]
    depth, tile = near.shape[1], act.shape[1]

    @pl.when(step == 0)
    def _():
        acc_d[...] = jnp.zeros_like(acc_d)
        acc_y[...] = jnp.zeros_like(acc_y)
        for i, (h_ref, d_ref) in enumerate(((near, dnear), (far, dfar))):
            h2[i * half : (i + 1) * half, :] = h_ref[...]
            d_out[i * half : (i + 1) * half, :] = d_ref[...]

    w1_tile = w1[...].reshape(depth, tile)
    w2_tile = jnp.concatenate(
        [
            jnp.concatenate(
                [w2[d, :, a * 128 : (a + 1) * 128] for d in range(w2.shape[0])], axis=1
            )
            for a in range(tile // 128)
        ],
        axis=0,
    )
    column = jnp.zeros((1, tile), f32)
    bias = small[6:7, pl.ds(pl.multiple_of(step * tile, 128), tile)]
    for i, (h_ref, d_ref) in enumerate(((near, dnear), (far, dfar))):
        block = slice(i * half, (i + 1) * half)
        pre = dot(h_ref[...], w1_tile) + bias
        d_act = dot(d_ref[...], w2_tile, NT)
        value, slope = gelu_parts(pre)
        value = value.astype(bf16)
        grad = (d_act * slope).astype(bf16)
        act[block, :] = value
        dpre[block, :] = grad
        column = column + jnp.sum(grad.astype(f32), axis=0, keepdims=True)
        acc_d[block, :] += dot(grad, w1_tile, NT)
        acc_y[block, :] += dot(value, w2_tile)
    bias_sum[...] = jnp.broadcast_to(column, bias_sum.shape)

    @pl.when(step == pl.num_programs(0) - 1)
    def _():
        dh_keep[...] = acc_d[0:half, :].astype(bf16)
        dh_send[...] = acc_d[half:, :].astype(bf16)
        y_keep[...] = acc_y[0:half, :].astype(bf16)
        y_send[...] = acc_y[half:, :].astype(bf16)


def project_kernel(att, wo, keep, send):
    half = keep.shape[0]
    for i, out in enumerate((keep, send)):
        out[...] = dot(att[i * half : (i + 1) * half, :], wo[...]).astype(bf16)


def norm_kernel(own, far, x, small, mid, h2):
    total = x[...].astype(f32) + own[...] + far[...].astype(f32) + small[4:5, :]
    mid[...] = total
    h2[...] = norm_rows(total, small[1:2, :], small[3:4, :]).astype(bf16)


def norm_back_rows(values, gain, grad):
    mean = jnp.mean(values, axis=-1, keepdims=True)
    centered = values - mean
    var = jnp.mean(centered * centered, axis=-1, keepdims=True)
    r = lax.rsqrt(var + norm_eps)
    xhat = centered * r
    f = grad * gain
    d_in = r * (
        f
        - jnp.mean(f, axis=-1, keepdims=True)
        - xhat * jnp.mean(f * xhat, axis=-1, keepdims=True)
    )
    return d_in, jnp.sum(grad * xhat, axis=0, keepdims=True), jnp.sum(grad, axis=0, keepdims=True)


def norm_back_kernel(row, own, far, values, beside, small, wide, *rest):
    sums = rest[-1]
    d_in, d_gain, d_shift = norm_back_rows(
        values[...].astype(f32), small[row : row + 1, :], own[...] + far[...].astype(f32)
    )
    total = beside[...].astype(f32) + d_in
    wide[...] = total
    parts = [d_gain, d_shift]
    if len(rest) > 1:
        rest[0][...] = total.astype(bf16)
        parts += [
            jnp.sum(total, axis=0, keepdims=True),
            jnp.sum(beside[...].astype(f32), axis=0, keepdims=True),
        ]
    parts.append(jnp.zeros((8 - len(parts), d_in.shape[1]), f32))
    sums[...] = jnp.concatenate(parts, axis=0)


def body(inputs, wqkv, qv_bias, wo, w1, b1, w2, gains, shifts, cotangent, span_lengths):
    slots, images, width_d = inputs.shape
    dp_size = lax.axis_size("dp")
    dp_index = lax.axis_index("dp")
    rank = lax.axis_index("tensor")
    rows = up(slots, 8)
    half, every = 2 * rows, 4 * rows
    width = wqkv.shape[2]
    heads, head_dim = qv_bias.shape[1], qv_bias.shape[2] * dp_size
    hidden = w1.shape[1]

    def apart(x):
        return jnp.pad(jnp.transpose(x, (1, 0, 2)), ((0, 0), (0, rows - slots), (0, 0)))

    x_own = apart(inputs)
    slot = jnp.arange(rows, dtype=jnp.int32)

    def used(k):
        return slot < lax.dynamic_index_in_dim(span_lengths, rank ^ k, keepdims=False)

    valid_own = used(0).astype(f32)[:, None]
    kmask = jnp.where(
        jnp.concatenate([used(0), used(2), used(1), used(3)]), 0.0, masked_score
    ).astype(f32)
    kmask_row, kmask_col = kmask[None, :], kmask[:, None]

    d_out = (apart(cotangent).astype(f32) * valid_own).astype(bf16)

    index = dp_index.astype(jnp.int32)[None]
    if dp_size == 8:
        small = jnp.concatenate(
            [
                gains,
                shifts,
                b1.reshape(1, -1),
                jnp.pad(qv_bias.reshape(1, -1), ((0, 0), (0, 128 - qv_bias.size))),
            ]
        )
        first = jnp.concatenate(
            [
                jnp.transpose(wqkv, (1, 0, 2)).reshape(-1, width),
                jnp.pad(small, ((0, 8), (0, width - 128))),
                jnp.transpose(wo.reshape(width // 128, 128, 128), (1, 0, 2)).reshape(128, width),
            ]
        )
        late = jnp.stack(
            [
                w1,
                jnp.transpose(w2.reshape(hidden // 128, 128, 128), (1, 0, 2)).reshape(128, hidden),
            ]
        )
        got = dp_blocks_begin(first)
        x_far, *got = lax.optimization_barrier((hop(x_own, "tensor", 2), *got))
        blocks = dp_blocks_end(first, got)
        d_out_far = hop(after(d_out, x_far), "tensor", 2)
        x_near, x_far = gather_core(x_own, after(x_far, blocks[3], blocks[5]), axis=1)
        mlp_weights = lax.all_gather(after(late, *got), "dp", axis=1, tiled=False)
        wqkv_full, wo_full, small_full = call(
            place_first,
            (((3, width_d, width), bf16), ((width, width_d), bf16), ((8, width_d), f32)),
            index,
            *blocks,
            scalars=1,
            nbytes=4 << 20,
            grid=(1,),
            vmem=60,
        )
    else:
        wqkv_full = jnp.transpose(lax.all_gather(wqkv, "dp", axis=0, tiled=True), (1, 0, 2))
        wo_full = lax.all_gather(wo, "dp", axis=1, tiled=True)
        w1_full = lax.all_gather(w1, "dp", axis=0, tiled=True).reshape(8, -1, hidden)
        w2_full = lax.all_gather(w2, "dp", axis=1, tiled=True)
        w2_full = jnp.transpose(
            w2_full.reshape(hidden // 128, 128, width_d // 128, 128), (2, 1, 0, 3)
        ).reshape(8, 128, hidden)
        mlp_weights = jnp.stack([w1_full, w2_full])
        qvb = lax.all_gather(qv_bias, "dp", axis=2, tiled=True).reshape(1, -1)
        small_full = jnp.concatenate(
            [
                lax.all_gather(jnp.concatenate([gains, shifts]), "dp", axis=1, tiled=True),
                lax.all_gather(b1, "dp", axis=1, tiled=True).reshape(1, hidden),
                jnp.pad(qvb, ((0, 0), (0, width_d - qvb.size))),
            ]
        ).astype(f32)
        x_near, x_far = gather_core(x_own, hop(x_own, "tensor", 2), axis=1)
        d_out_far = hop(d_out, "tensor", 2)


    def image_of(i, n):
        return pl.BlockSpec((None, n, width_d), lambda *_: (i, 0, 0))

    kept, parts, mids = [], [], []

    def norm_of(i):
        own, far = parts[i]
        if i == 1:
            own = after(own, parts[2][1])
        return call(
            norm_kernel,
            (((rows, width_d), f32), ((rows, width_d), bf16)),
            own,
            hop(far, "tensor", 2),
            x_own[i],
            small_full,
            nbytes=2 << 20,
        )

    for i in range(images):
        near = x_near
        if i == 1:
            near = after(near, d_out_far)
        if i == 2:
            near = after(near, parts[0][1])
        h1, qkv, att, lse = call(
            attention_kernel,
            (
                ((every, width_d), bf16),
                ((every, 3 * width), bf16),
                ((every, width), bf16),
                ((every, 128), f32),
            ),
            near,
            x_far,
            wqkv_full,
            small_full,
            kmask_row,
            specs={0: image_of(i, half), 1: image_of(i, half)},
            grid=(1,),
            flops=2 * every * width_d * 3 * width + 8 * every * every * 256,
            nbytes=8 << 20,
        )
        kept.append((h1, qkv, att, lse))
        if i == 2:
            mids.append(norm_of(0))
            att = after(att, mids[0][0])
        keep, send = call(
            project_kernel,
            (((half, width_d), bf16), ((half, width_d), bf16)),
            att,
            wo_full,
            flops=2 * every * width * width_d,
            nbytes=2 << 20,
        )
        parts.append(scatter_core(keep, send))
    d_near, d_far = gather_core(d_out, d_out_far, axis=1)
    mids.append(norm_of(1))
    mids.append(norm_of(2))
    h2s = [gather_tokens(h2) for _, h2 in mids]
    mids = [mid for mid, _ in mids]

    tile = min(512, hidden)
    token = pl.BlockSpec((half, width_d), lambda j: (0, 0))
    mlp, parts, y_parts = [], [], []
    for i in range(images):
        near, far = h2s[i]
        if i < 2:
            near = after(near, mids[i + 1])
        else:
            near = after(near, parts[0][1])
        *grads, dh_keep, dh_send, y_keep, y_send = call(
            mlp_kernel,
            (
                ((every, hidden), bf16, pl.BlockSpec((every, tile), lambda j: (0, j))),
                ((every, hidden), bf16, pl.BlockSpec((every, tile), lambda j: (0, j))),
                ((every, width_d), bf16, pl.BlockSpec((every, width_d), lambda j: (0, 0))),
                ((every, width_d), bf16, pl.BlockSpec((every, width_d), lambda j: (0, 0))),
                ((8, hidden), f32, pl.BlockSpec((8, tile), lambda j: (0, j))),
                ((half, width_d), bf16, token),
                ((half, width_d), bf16, token),
                ((half, width_d), bf16, token),
                ((half, width_d), bf16, token),
            ),
            near,
            far,
            d_near,
            d_far,
            mlp_weights,
            mlp_weights,
            small_full,
            specs={
                0: token,
                1: token,
                2: image_of(i, half),
                3: image_of(i, half),
                4: pl.BlockSpec((None, 8, 128, tile), lambda j: (0, 0, 0, j)),
                5: pl.BlockSpec((None, 8, 128, tile), lambda j: (1, 0, 0, j)),
                6: pl.BlockSpec((8, width_d), lambda j: (0, 0)),
            },
            vmem=48,
            flops=8 * every * width_d * hidden,
            nbytes=14 << 20,
            grid=(hidden // tile,),
            scratch_shapes=[pltpu.VMEM((every, width_d), f32), pltpu.VMEM((every, width_d), f32)],
        )
        mlp.append(grads)
        parts.append(scatter_core(dh_keep, dh_send))
        y_parts.append((y_keep, y_send))
    d_mids, d_mid_all, sums = [], [], []
    for i in range(images):
        own, far = parts[i]
        if i == 0:
            own = after(own, parts[1][1])
        if i == 1:
            own = after(own, parts[2][1])
        d_mid, d_mid_b, part = call(
            functools.partial(norm_back_kernel, 1),
            (((rows, width_d), f32), ((rows, width_d), bf16), ((8, width_d), f32)),
            own,
            hop(far, "tensor", 2),
            mids[i],
            d_out[i],
            small_full,
            nbytes=3 << 20,
        )
        d_mids.append(d_mid)
        sums.append(part)
        d_mid_all.append(gather_tokens(d_mid_b))

    def rows_product(a, b):
        return sum(dot(x, y, TN) for x, y in zip(a, b, strict=True))

    act, dpre, h2_in, d_out_in, b1_sums = zip(*mlp, strict=True)
    dpre = lax.optimization_barrier((*dpre, d_mids[0], parts[2][1]))[:images]
    grad_w1 = rows_product(h2_in, dpre).astype(bf16)
    act = lax.optimization_barrier((*act, d_mids[1], grad_w1))[:images]
    grad_w2 = rows_product(act, d_out_in).astype(bf16)
    grad_b1 = sum(x[0] for x in b1_sums)
    if dp_size == 8:
        w1_own = lax.psum_scatter(grad_w1, "dp", scatter_dimension=0, tiled=True)
        late = call(
            pack_columns,
            (((2, hidden, 128), bf16),) * 4,
            index,
            grad_w2,
            scalars=1,
            nbytes=8 << 20,
        )
        late_far = hop(late[0], "dp", 1)
    else:
        late = grad_w2

    y_parts = [scatter_core(after(k, d_mids[0]), s) for k, s in y_parts]
    y_own, y_far = (jnp.stack(p) for p in zip(*y_parts, strict=True))
    y_far = hop(after(y_far, d_mid_all[2][0]), "tensor", 2)

    back, parts = [], []
    for i in range(images):
        h1, qkv, att, lse = kept[i]
        near, far = d_mid_all[i]
        if i == 0:
            near = after(near, late[0])
        if i == 1:
            near = after(near, d_mids[2])
        if i == 2:
            near = after(near, parts[0][1])
            if dp_size == 8:
                w2_sums = dp_reduce_begin(*late, late_far, back[0][0])
        dqkv, d_mid_in, bias_sum, dh_keep, dh_send = call(
            attention_back_kernel,
            (
                ((every, 3 * width), bf16),
                ((every, width_d), bf16),
                ((8, 3 * width), f32),
                ((half, width_d), bf16),
                ((half, width_d), bf16),
            ),
            near,
            far,
            wo_full,
            wqkv_full,
            qkv,
            att,
            lse,
            kmask_col,
            flops=2 * every * width_d * 4 * width + 20 * every * every * 256,
            nbytes=8 << 20,
            scratch_shapes=[pltpu.VMEM((every, width), bf16)],
        )
        back.append((dqkv, d_mid_in, bias_sum))
        parts.append(scatter_core(dh_keep, dh_send))

    dqkv, d_mid_in, bias_sums = zip(*back, strict=True)
    grad_wqkv = rows_product([k[0] for k in kept], dqkv)
    grad_wo = rows_product([k[2] for k in kept], d_mid_in)
    bias_sums = sum(x[0] for x in bias_sums)
    head_bias = jnp.concatenate([bias_sums[:width], bias_sums[2 * width :]])
    if dp_size == 8:
        block = (128, 3 * width + width)
        last = call(
            pack_last,
            (((2, *block), bf16),) * 4,
            index,
            after(grad_wqkv.astype(bf16), y_far),
            grad_wo.astype(bf16),
            scalars=1,
            nbytes=8 << 20,
        )
        last_sums = dp_reduce_begin(*last, hop(last[0], "dp", 1))
        last_far = dp_reduce_far(last_sums, bf16, (6, 4))
        w2_far = dp_reduce_far(w2_sums, bf16, (6, 4, 2))
    grad_in, sums1 = [], []
    for i in range(images):
        own, far = parts[i]
        d_in, part = call(
            functools.partial(norm_back_kernel, 0),
            (((rows, width_d), f32), ((8, width_d), f32)),
            own,
            hop(far, "tensor", 2),
            x_own[i],
            d_mids[i],
            small_full,
            nbytes=3 << 20,
        )
        grad_in.append(d_in)
        sums1.append(part)
    outs = jnp.stack(mids) + y_own + y_far.astype(f32) + small_full[5]
    outs = (outs * valid_own).astype(bf16)
    sum1, sum2 = sum(sums1), sum(sums)
    small_sums = jnp.stack(
        [sum1[0], sum2[0], sum1[1], sum2[1], sum2[2], sum2[3], sum2[7], sum2[7]]
    )
    if dp_size == 8:
        w1_own = w1_own.astype(f32)
        w2_own = w2_sums[0] + sum(w2_far)
        small_sums = small_sums + hop(small_sums, "tensor", 1)
        small_sums = small_sums + hop(small_sums, "tensor", 2)
        small_sums = after(small_sums, *last_far, w2_own)
        send, keep = call(
            pack_small,
            (((4, 8, 128), f32),) * 2,
            index,
            small_sums,
            grad_b1[None, :],
            head_bias[None, :],
            scalars=1,
        )
        tiny = keep + hop(send, "dp", 1)
        tiny_far = dp_reduce_far({2 * k: tiny[k] for k in range(4)}, f32, (6, 4, 2))
        last_near = dp_reduce_far(last_sums, bf16, (2,))[0]
        own = last_sums[0] + sum(last_far) + last_near
        wqkv_own = own[:, : 3 * width].reshape(128, 3, width)
        wo_own = jnp.transpose(
            own[:, 3 * width :].reshape(128, width // 128, 128), (1, 0, 2)
        ).reshape(wo.shape)
        got = after(tiny[0], last_near) + sum(tiny_far)
        part = got[:6]
        b1_own = got[6].reshape(b1.shape)
        qvb_own = got[7, : qv_bias.size].reshape(qv_bias.shape)
    else:
        scatter = functools.partial(lax.psum_scatter, axis_name="dp", tiled=True)
        w2_own = scatter(grad_w2.astype(f32), scatter_dimension=1)
        w1_own = scatter(grad_w1.astype(f32), scatter_dimension=0)
        wo_own = scatter(grad_wo, scatter_dimension=1)
        wqkv_own = scatter(grad_wqkv, scatter_dimension=0).reshape(wqkv.shape)
        b1_own = scatter(grad_b1.reshape(b1.shape[0], -1), scatter_dimension=1)
        qvb_own = scatter(head_bias.reshape(2, heads, head_dim), scatter_dimension=2)
        part = lax.psum(scatter(small_sums[:6], scatter_dimension=1), "tensor")

    def together(parts):
        return jnp.transpose(parts[:, :slots], (1, 0, 2))

    return (
        together(outs),
        together(jnp.stack(grad_in)),
        wqkv_own.reshape(wqkv.shape),
        qvb_own,
        wo_own,
        w1_own,
        b1_own,
        w2_own,
        part[:2],
        part[2:],
    )


def solution(mesh):
    return jax.shard_map(
        body,
        mesh=mesh,
        in_specs=(
            P("tensor", "dp", None),
            P("dp", None, "tensor"),
            P(None, "tensor", "dp"),
            P("tensor", "dp"),
            P("dp", "tensor"),
            P("tensor", "dp"),
            P("tensor", "dp"),
            P(None, "dp"),
            P(None, "dp"),
            P("tensor", "dp", None),
            P(),
        ),
        out_specs=(
            P("tensor", "dp", None),
            P("tensor", "dp", None),
            P("dp", None, "tensor"),
            P(None, "tensor", "dp"),
            P("tensor", "dp"),
            P("dp", "tensor"),
            P("tensor", "dp"),
            P("tensor", "dp"),
            P(None, "dp"),
            P(None, "dp"),
        ),
        check_vma=False,
    )
```

```python
import functools

import jax
import jax.numpy as jnp
from jax import lax
from jax.experimental import pallas as pl
from jax.experimental.pallas import tpu as pltpu
from jax.sharding import PartitionSpec as P

norm_eps = 1e-06
masked_score = -1e30
f32 = jnp.float32
bf16 = jnp.bfloat16
NT = (((1,), (1,)), ((), ()))
TN = (((0,), (0,)), ((), ()))
NN = (((1,), (0,)), ((), ()))


def dot(a, b, dims=NN):
    return lax.dot_general(a, b, dims, preferred_element_type=f32)


def up(size, step):
    return -(-size // step) * step


cost_part = 512


def call(kernel, outs, *args, vmem=40, flops=0, nbytes=0, scalars=0, **kw):
    whole = pl.BlockSpec(memory_space=pltpu.VMEM)

    def spec(i, x):
        if i < scalars:
            return pl.BlockSpec(memory_space=pltpu.SMEM)
        if "grid" not in kw:
            return whole
        return pl.BlockSpec(x.shape, lambda *_: (0,) * x.ndim)

    in_specs = [spec(i, x) for i, x in enumerate(args)]
    return pl.pallas_call(
        kernel,
        out_shape=tuple(jax.ShapeDtypeStruct(o[0], o[1]) for o in outs),
        in_specs=in_specs,
        out_specs=(whole,) * len(outs),
        compiler_params=pltpu.CompilerParams(vmem_limit_bytes=vmem << 20),
        cost_estimate=pl.CostEstimate(
            flops=flops // cost_part, bytes_accessed=nbytes // cost_part, transcendentals=0
        ),
        **kw,
    )(*args)


def after(x, *deps):
    return lax.optimization_barrier((x, *deps))[0]


def hop(x, axis, k):
    size = lax.axis_size(axis)
    return lax.ppermute(x, axis, [(i, i ^ k) for i in range(size)])


def gather_core(x, far, axis=0):
    near = jnp.concatenate([x, far], axis=axis)
    return near, hop(near, "tensor", 1)


def gather_tokens(x):
    return gather_core(x, hop(x, "tensor", 2))


def scatter_core(keep, send):
    rows = keep.shape[-2] // 2
    got = hop(send, "tensor", 1)
    own = keep[..., :rows, :].astype(f32) + got[..., :rows, :].astype(f32)
    far = keep[..., rows:, :].astype(f32) + got[..., rows:, :].astype(f32)
    return own, far.astype(bf16)


def dp_blocks_begin(x):
    return [hop(x, "dp", k) for k in (1, 2, 4, 6)]


def dp_blocks_end(x, got):
    side, *far = got
    near = [x, *far]
    other = [side, *(hop(b, "dp", 1) for b in far)]
    return [b for pair in zip(near, other, strict=True) for b in pair]


def dp_reduce_begin(send_far, send_near, keep_far, keep_near, far, *deps):
    if deps:
        far = after(far, *deps)
    near = hop(after(send_near, far), "dp", 1).astype(f32)
    far = keep_far.astype(f32) + far.astype(f32)
    near = keep_near.astype(f32) + near
    return {6: far[0], 4: far[1], 2: near[0], 0: near[1]}


def dp_reduce_far(sums, kind, offsets):
    return [hop(sums[k].astype(kind), "dp", k).astype(f32) for k in offsets]


def spread(at, width):
    t = lax.broadcasted_iota(jnp.int32, (128, width), 1)
    source = lax.broadcasted_iota(jnp.int32, (128, width), 0)
    return ((t // 8) % 8 == at) & (source == (t // 64) * 8 + t % 8)


def place_first(index, *refs):
    *blocks, wqkv, wo, small = refs
    width = wqkv.shape[2]
    rows = wqkv.shape[1] // 8
    total = jnp.zeros((8, small.shape[1]), f32)
    for k, block in enumerate(blocks):
        at = index[0] ^ k
        here = pl.ds(pl.multiple_of(at * 128, 128), 128)
        for c in range(3):
            wqkv[c, here, :] = block[c * rows : (c + 1) * rows, :]
        for a in range(width // 128):
            wo[a * 128 : (a + 1) * 128, here] = block[
                3 * rows + 16 : 4 * rows + 16, a * 128 : (a + 1) * 128
            ]
        part = block[3 * rows : 3 * rows + 16, 0:128][0:8]
        small[0:6, here] = part[0:6].astype(f32)
        total = total + dot(part, spread(at, small.shape[1]).astype(f32).astype(bf16))
    small[6:8, :] = total[6:8]


def pack_small(index, sums, hidden_bias, head_bias, send, keep):
    width = sums.shape[1]
    both = jnp.concatenate(
        [
            hidden_bias[...],
            jnp.pad(head_bias[...], ((0, 0), (0, width - head_bias.shape[1]))),
            jnp.zeros((6, width), f32),
        ],
        axis=0,
    )
    for k in range(8):
        at = index[0] ^ k
        out = (keep, send)[k % 2].at[k // 2]
        here = pl.ds(pl.multiple_of(at * 128, 128), 128)
        out[0:6, :] = sums[0:6, here]
        out[6:8, :] = lax.dot_general(
            both,
            spread(at, width).astype(f32),
            NT,
            precision=lax.Precision.HIGHEST,
            preferred_element_type=f32,
        )[0:2]


def pack_columns(index, grad, *outs):
    for n, k in enumerate((6, 4, 2, 0)):
        for m, out in ((k + 1, outs[n // 2].at[n % 2]), (k, outs[2 + n // 2].at[n % 2])):
            at = index[0] ^ m
            out[...] = grad[:, pl.ds(pl.multiple_of(at * 128, 128), 128)]


def pack_last(index, g_qkv, g_o, *outs):
    for n, k in enumerate((6, 4, 2, 0)):
        for m, out in ((k + 1, outs[n // 2].at[n % 2]), (k, outs[2 + n // 2].at[n % 2])):
            at = index[0] ^ m
            here = pl.ds(pl.multiple_of(at * 128, 128), 128)
            out[:, 0 : g_qkv.shape[1]] = g_qkv[here, :].astype(out.dtype)
            for a in range(g_o.shape[0] // 128):
                lo = g_qkv.shape[1] + a * 128
                out[:, lo : lo + 128] = g_o[a * 128 : (a + 1) * 128, here].astype(out.dtype)


def norm_rows(x, gain, shift):
    mean = jnp.mean(x, axis=-1, keepdims=True)
    centered = x - mean
    var = jnp.mean(centered * centered, axis=-1, keepdims=True)
    return centered * lax.rsqrt(var + norm_eps) * gain + shift


def attention_kernel(image, near, far, wqkv, small, kmask, h1, qkv, att, lse):
    half = near.shape[1]
    width = wqkv.shape[2]
    for i, ref in enumerate((near, far)):
        x = ref[image].astype(f32)
        h1[i * half : (i + 1) * half, :] = norm_rows(x, small[0:1, :], small[2:3, :]).astype(bf16)
    for c in range(3):
        out = dot(h1[...], wqkv[c])
        if c != 1:
            out = out + small[7:8, (c // 2) * width : (c // 2 + 1) * width]
        out = out.astype(bf16)
        if c == 0:
            out = out * bf16(0.125)
        qkv[:, c * width : (c + 1) * width] = out
    lane = lax.broadcasted_iota(jnp.int32, (1, 128), 1)
    lane_f = lane
    lse_parts = [jnp.zeros((half, 128), f32) for _ in range(2)]
    for p in range(width // 128):
        keys = qkv[:, width + p * 128 : width + (p + 1) * 128]
        vals = qkv[:, 2 * width + p * 128 : 2 * width + (p + 1) * 128]
        outs = [jnp.zeros((half, 128), f32) for _ in range(2)]
        for h in range(2):
            mine = (lane >= 64 * h) & (lane < 64 * h + 64)
            k_h = jnp.where(mine, keys, bf16(0))
            v_h = jnp.where(mine, vals, bf16(0))
            for b in range(2):
                q = qkv[b * half : (b + 1) * half, p * 128 : (p + 1) * 128]
                s = dot(q, k_h, NT) + kmask[...]
                top = jnp.max(s, axis=-1, keepdims=True)
                e = jnp.exp(s - top)
                total = jnp.sum(e, axis=-1, keepdims=True)
                outs[b] = outs[b] + dot(e.astype(bf16), v_h) / total
                lse_parts[b] = jnp.where(
                    lane_f == 2 * p + h, top + jnp.log(total), lse_parts[b]
                )
        for b in range(2):
            att[b * half : (b + 1) * half, p * 128 : (p + 1) * 128] = outs[b].astype(bf16)
    for b in range(2):
        lse[b * half : (b + 1) * half, :] = lse_parts[b]


def attention_back_kernel(
    near, far, wo, wqkv, qkv, att, lse, kmask, dqkv, d_mid, bias_sum, dh_keep, dh_send, d_att
):
    half = near.shape[0]
    rows = 2 * half
    width = wo.shape[0]
    for i, ref in enumerate((near, far)):
        d_mid[i * half : (i + 1) * half, :] = ref[...]
        d_att[i * half : (i + 1) * half, :] = dot(ref[...], wo[...], NT).astype(bf16)
    prod = d_att[...].astype(f32) * att[...].astype(f32)
    heads = width // 64
    pick_d = (
        lax.broadcasted_iota(jnp.int32, (8, width), 1) // 64
        == lax.broadcasted_iota(jnp.int32, (8, width), 0)
    ).astype(f32)
    pick_l = (
        lax.broadcasted_iota(jnp.int32, (8, 128), 1)
        == lax.broadcasted_iota(jnp.int32, (8, 128), 0)
    ).astype(f32)
    row_dot = lax.dot_general(
        pick_d, prod, NT, precision=lax.Precision.HIGHEST, preferred_element_type=f32
    )
    row_lse = lax.dot_general(
        pick_l, lse[...], NT, precision=lax.Precision.HIGHEST, preferred_element_type=f32
    )
    lane = lax.broadcasted_iota(jnp.int32, (1, 128), 1)
    for p in range(width // 128):
        cols = slice(p * 128, (p + 1) * 128)
        q = qkv[:, p * 128 : (p + 1) * 128]
        d_o = d_att[:, cols]
        dq = jnp.zeros((rows, 128), f32)
        for b in range(2):
            block = slice(b * half, (b + 1) * half)
            keys = qkv[block, width + p * 128 : width + (p + 1) * 128]
            vals = qkv[block, 2 * width + p * 128 : 2 * width + (p + 1) * 128]
            dk = jnp.zeros((half, 128), f32)
            dv = jnp.zeros((half, 128), f32)
            for h in range(2):
                mine = (lane >= 64 * h) & (lane < 64 * h + 64)
                k_h = jnp.where(mine, keys, bf16(0))
                v_h = jnp.where(mine, vals, bf16(0))
                at = 2 * p + h
                s = dot(k_h, q, NT) + kmask[block, :]
                probs = jnp.exp(s - row_lse[at : at + 1, :])
                d_p = dot(v_h, d_o, NT)
                d_s = (probs * (d_p - row_dot[at : at + 1, :])).astype(bf16)
                dv = dv + dot(probs.astype(bf16), jnp.where(mine, d_o, bf16(0)))
                dk = dk + dot(d_s, jnp.where(mine, q, bf16(0)))
                dq = dq + dot(d_s, k_h, TN)
            dqkv[block, width + p * 128 : width + (p + 1) * 128] = dk.astype(bf16)
            dqkv[block, 2 * width + p * 128 : 2 * width + (p + 1) * 128] = dv.astype(bf16)
        dqkv[:, p * 128 : (p + 1) * 128] = (dq * 0.125).astype(bf16)
    bias_sum[...] = jnp.broadcast_to(
        jnp.sum(dqkv[...].astype(f32), axis=0, keepdims=True), bias_sum.shape
    )
    for i, ref in enumerate((dh_keep, dh_send)):
        block = slice(i * half, (i + 1) * half)
        total = dot(dqkv[block, 0:width], wqkv[0], NT)
        for c in (1, 2):
            total = total + dot(dqkv[block, c * width : (c + 1) * width], wqkv[c], NT)
        ref[...] = total.astype(bf16)


def gelu_parts(u):
    e = jnp.exp(-0.5 * u * u)
    t = 1.0 / (1.0 + (0.3275911 * 0.7071067811865476) * jnp.abs(u))
    poly = t * (
        0.5 * 0.254829592
        + t
        * (
            0.5 * -0.284496736
            + t * (0.5 * 1.421413741 + t * (0.5 * -1.453152027 + t * (0.5 * 1.061405429)))
        )
    )
    tail = poly * e
    phi_sum = jnp.where(u >= 0, 1.0 - tail, tail)
    return u * phi_sum, phi_sum + u * (e * 0.3989422804014327)


def mlp_kernel(
    image,
    near,
    far,
    dnear,
    dfar,
    weights,
    small,
    act,
    dpre,
    h2,
    d_out,
    bias_sum,
    dh_keep,
    dh_send,
    y_keep,
    y_send,
):
    half, depth = near.shape
    hidden = act.shape[1]
    w1 = weights[0].reshape(depth, hidden)
    w2 = jnp.concatenate(
        [
            jnp.concatenate(
                [weights[1, d, :, a * 128 : (a + 1) * 128] for d in range(depth // 128)], axis=1
            )
            for a in range(hidden // 128)
        ],
        axis=0,
    )
    column = jnp.zeros((1, hidden), f32)
    for i, (h_ref, d_ref, dh, y) in enumerate(
        ((near, dnear, dh_keep, y_keep), (far, dfar, dh_send, y_send))
    ):
        block = slice(i * half, (i + 1) * half)
        h = h_ref[...]
        d = d_ref[image]
        h2[block, :] = h
        d_out[block, :] = d
        value, slope = gelu_parts(dot(h, w1) + small[6:7, :])
        value = value.astype(bf16)
        grad = (dot(d, w2, NT) * slope).astype(bf16)
        act[block, :] = value
        dpre[block, :] = grad
        column = column + jnp.sum(grad.astype(f32), axis=0, keepdims=True)
        dh[...] = dot(grad, w1, NT).astype(bf16)
        y[...] = dot(value, w2).astype(bf16)
    bias_sum[...] = jnp.broadcast_to(column, bias_sum.shape)


def project_kernel(att, wo, keep, send):
    half = keep.shape[0]
    for i, out in enumerate((keep, send)):
        out[...] = dot(att[i * half : (i + 1) * half, :], wo[...]).astype(bf16)


def norm_kernel(own, far, x, small, mid, h2):
    total = x[...].astype(f32) + own[...] + far[...].astype(f32) + small[4:5, :]
    mid[...] = total
    h2[...] = norm_rows(total, small[1:2, :], small[3:4, :]).astype(bf16)


def norm_back_rows(values, gain, grad):
    mean = jnp.mean(values, axis=-1, keepdims=True)
    centered = values - mean
    var = jnp.mean(centered * centered, axis=-1, keepdims=True)
    r = lax.rsqrt(var + norm_eps)
    xhat = centered * r
    f = grad * gain
    d_in = r * (
        f
        - jnp.mean(f, axis=-1, keepdims=True)
        - xhat * jnp.mean(f * xhat, axis=-1, keepdims=True)
    )
    return d_in, jnp.sum(grad * xhat, axis=0, keepdims=True), jnp.sum(grad, axis=0, keepdims=True)


def norm_back_kernel(row, own, far, values, beside, small, wide, *rest):
    sums = rest[-1]
    d_in, d_gain, d_shift = norm_back_rows(
        values[...].astype(f32), small[row : row + 1, :], own[...] + far[...].astype(f32)
    )
    total = beside[...].astype(f32) + d_in
    wide[...] = total
    parts = [d_gain, d_shift]
    if len(rest) > 1:
        rest[0][...] = total.astype(bf16)
        parts += [
            jnp.sum(total, axis=0, keepdims=True),
            jnp.sum(beside[...].astype(f32), axis=0, keepdims=True),
        ]
    parts.append(jnp.zeros((8 - len(parts), d_in.shape[1]), f32))
    sums[...] = jnp.concatenate(parts, axis=0)


def body(inputs, wqkv, qv_bias, wo, w1, b1, w2, gains, shifts, cotangent, span_lengths):
    slots, images, width_d = inputs.shape
    dp_size = lax.axis_size("dp")
    dp_index = lax.axis_index("dp")
    rank = lax.axis_index("tensor")
    rows = up(slots, 8)
    half, every = 2 * rows, 4 * rows
    width = wqkv.shape[2]
    heads, head_dim = qv_bias.shape[1], qv_bias.shape[2] * dp_size
    hidden = w1.shape[1]

    def apart(x):
        return jnp.pad(jnp.transpose(x, (1, 0, 2)), ((0, 0), (0, rows - slots), (0, 0)))

    x_own = apart(inputs)
    slot = jnp.arange(rows, dtype=jnp.int32)

    def used(k):
        return slot < lax.dynamic_index_in_dim(span_lengths, rank ^ k, keepdims=False)

    valid_own = used(0).astype(f32)[:, None]
    kmask = jnp.where(
        jnp.concatenate([used(0), used(2), used(1), used(3)]), 0.0, masked_score
    ).astype(f32)
    kmask_row, kmask_col = kmask[None, :], kmask[:, None]

    d_out = (apart(cotangent).astype(f32) * valid_own).astype(bf16)

    index = dp_index.astype(jnp.int32)[None]
    if dp_size == 8:
        small = jnp.concatenate(
            [
                gains,
                shifts,
                b1.reshape(1, -1),
                jnp.pad(qv_bias.reshape(1, -1), ((0, 0), (0, 128 - qv_bias.size))),
            ]
        )
        first = jnp.concatenate(
            [
                jnp.transpose(wqkv, (1, 0, 2)).reshape(-1, width),
                jnp.pad(small, ((0, 8), (0, width - 128))),
                jnp.transpose(wo.reshape(width // 128, 128, 128), (1, 0, 2)).reshape(128, width),
            ]
        )
        late = jnp.stack(
            [
                w1,
                jnp.transpose(w2.reshape(hidden // 128, 128, 128), (1, 0, 2)).reshape(128, hidden),
            ]
        )
        got = dp_blocks_begin(first)
        x_far, *got = lax.optimization_barrier((hop(x_own, "tensor", 2), *got))
        blocks = dp_blocks_end(first, got)
        d_out_far = hop(after(d_out, x_far), "tensor", 2)
        x_near, x_far = gather_core(x_own, after(x_far, blocks[3], blocks[5]), axis=1)
        mlp_weights = lax.all_gather(after(late, *got), "dp", axis=1, tiled=False)
        wqkv_full, wo_full, small_full = call(
            place_first,
            (((3, width_d, width), bf16), ((width, width_d), bf16), ((8, width_d), f32)),
            index,
            *blocks,
            scalars=1,
            nbytes=4 << 20,
            grid=(1,),
            vmem=60,
        )
    else:
        wqkv_full = jnp.transpose(lax.all_gather(wqkv, "dp", axis=0, tiled=True), (1, 0, 2))
        wo_full = lax.all_gather(wo, "dp", axis=1, tiled=True)
        w1_full = lax.all_gather(w1, "dp", axis=0, tiled=True).reshape(8, -1, hidden)
        w2_full = lax.all_gather(w2, "dp", axis=1, tiled=True)
        w2_full = jnp.transpose(
            w2_full.reshape(hidden // 128, 128, width_d // 128, 128), (2, 1, 0, 3)
        ).reshape(8, 128, hidden)
        mlp_weights = jnp.stack([w1_full, w2_full])
        qvb = lax.all_gather(qv_bias, "dp", axis=2, tiled=True).reshape(1, -1)
        small_full = jnp.concatenate(
            [
                lax.all_gather(jnp.concatenate([gains, shifts]), "dp", axis=1, tiled=True),
                lax.all_gather(b1, "dp", axis=1, tiled=True).reshape(1, hidden),
                jnp.pad(qvb, ((0, 0), (0, width_d - qvb.size))),
            ]
        ).astype(f32)
        x_near, x_far = gather_core(x_own, hop(x_own, "tensor", 2), axis=1)
        d_out_far = hop(d_out, "tensor", 2)


    kept, parts, mids = [], [], []

    def norm_of(i):
        own, far = parts[i]
        if i == 1:
            own = after(own, parts[2][1])
        return call(
            norm_kernel,
            (((rows, width_d), f32), ((rows, width_d), bf16)),
            own,
            hop(far, "tensor", 2),
            x_own[i],
            small_full,
            nbytes=2 << 20,
        )

    for i in range(images):
        near = x_near
        if i == 1:
            near = after(near, d_out_far)
        if i == 2:
            near = after(near, parts[0][1])
        h1, qkv, att, lse = call(
            functools.partial(attention_kernel, i),
            (
                ((every, width_d), bf16),
                ((every, 3 * width), bf16),
                ((every, width), bf16),
                ((every, 128), f32),
            ),
            near,
            x_far,
            wqkv_full,
            small_full,
            kmask_row,
            vmem=24,
            flops=2 * every * width_d * 3 * width + 8 * every * every * 256,
            nbytes=8 << 20,
        )
        kept.append((h1, qkv, att, lse))
        if i == 2:
            mids.append(norm_of(0))
            att = after(att, mids[0][0])
        keep, send = call(
            project_kernel,
            (((half, width_d), bf16), ((half, width_d), bf16)),
            att,
            wo_full,
            flops=2 * every * width * width_d,
            nbytes=2 << 20,
        )
        parts.append(scatter_core(keep, send))
    d_near, d_far = gather_core(d_out, d_out_far, axis=1)
    mids.append(norm_of(1))
    mids.append(norm_of(2))
    h2s = [gather_tokens(h2) for _, h2 in mids]
    mids = [mid for mid, _ in mids]

    mlp, parts, y_parts = [], [], []
    for i in range(images):
        near, far = h2s[i]
        if i < 2:
            near = after(near, mids[i + 1])
        else:
            near = after(near, parts[0][1])
        *grads, dh_keep, dh_send, y_keep, y_send = call(
            functools.partial(mlp_kernel, i),
            (
                ((every, hidden), bf16),
                ((every, hidden), bf16),
                ((every, width_d), bf16),
                ((every, width_d), bf16),
                ((8, hidden), f32),
                ((half, width_d), bf16),
                ((half, width_d), bf16),
                ((half, width_d), bf16),
                ((half, width_d), bf16),
            ),
            near,
            far,
            d_near,
            d_far,
            mlp_weights,
            small_full,
            vmem=36,
            flops=8 * every * width_d * hidden,
            nbytes=14 << 20,
        )
        mlp.append(grads)
        parts.append(scatter_core(dh_keep, dh_send))
        y_parts.append((y_keep, y_send))
    d_mids, d_mid_all, sums = [], [], []
    for i in range(images):
        own, far = parts[i]
        if i == 0:
            own = after(own, parts[1][1])
        if i == 1:
            own = after(own, parts[2][1])
        d_mid, d_mid_b, part = call(
            functools.partial(norm_back_kernel, 1),
            (((rows, width_d), f32), ((rows, width_d), bf16), ((8, width_d), f32)),
            own,
            hop(far, "tensor", 2),
            mids[i],
            d_out[i],
            small_full,
            nbytes=3 << 20,
        )
        d_mids.append(d_mid)
        sums.append(part)
        d_mid_all.append(gather_tokens(d_mid_b))

    def rows_product(a, b):
        return sum(dot(x, y, TN) for x, y in zip(a, b, strict=True))

    act, dpre, h2_in, d_out_in, b1_sums = zip(*mlp, strict=True)
    dpre = lax.optimization_barrier((*dpre, d_mids[0], parts[2][1]))[:images]
    grad_w1 = rows_product(h2_in, dpre).astype(bf16)
    act = lax.optimization_barrier((*act, d_mids[1], grad_w1))[:images]
    grad_w2 = rows_product(act, d_out_in).astype(bf16)
    grad_b1 = sum(x[0] for x in b1_sums)
    if dp_size == 8:
        w1_own = lax.psum_scatter(grad_w1, "dp", scatter_dimension=0, tiled=True)
        late = call(
            pack_columns,
            (((2, hidden, 128), bf16),) * 4,
            index,
            grad_w2,
            scalars=1,
            nbytes=8 << 20,
        )
        late_far = hop(late[0], "dp", 1)
    else:
        late = grad_w2

    y_parts = [scatter_core(after(k, d_mids[0]), s) for k, s in y_parts]
    y_own, y_far = (jnp.stack(p) for p in zip(*y_parts, strict=True))
    y_far = hop(after(y_far, d_mid_all[2][0]), "tensor", 2)

    back, parts = [], []
    for i in range(images):
        h1, qkv, att, lse = kept[i]
        near, far = d_mid_all[i]
        if i == 0:
            near = after(near, late[0])
        if i == 1:
            near = after(near, d_mids[2])
        if i == 2:
            near = after(near, parts[0][1])
            if dp_size == 8:
                w2_sums = dp_reduce_begin(*late, late_far, back[0][0])
        dqkv, d_mid_in, bias_sum, dh_keep, dh_send = call(
            attention_back_kernel,
            (
                ((every, 3 * width), bf16),
                ((every, width_d), bf16),
                ((8, 3 * width), f32),
                ((half, width_d), bf16),
                ((half, width_d), bf16),
            ),
            near,
            far,
            wo_full,
            wqkv_full,
            qkv,
            att,
            lse,
            kmask_col,
            vmem=24,
            flops=2 * every * width_d * 4 * width + 20 * every * every * 256,
            nbytes=8 << 20,
            scratch_shapes=[pltpu.VMEM((every, width), bf16)],
        )
        back.append((dqkv, d_mid_in, bias_sum))
        parts.append(scatter_core(dh_keep, dh_send))

    dqkv, d_mid_in, bias_sums = zip(*back, strict=True)
    grad_wqkv = rows_product([k[0] for k in kept], dqkv)
    grad_wo = rows_product([k[2] for k in kept], d_mid_in)
    bias_sums = sum(x[0] for x in bias_sums)
    head_bias = jnp.concatenate([bias_sums[:width], bias_sums[2 * width :]])
    if dp_size == 8:
        block = (128, 3 * width + width)
        last = call(
            pack_last,
            (((2, *block), bf16),) * 4,
            index,
            after(grad_wqkv.astype(bf16), y_far),
            grad_wo.astype(bf16),
            scalars=1,
            nbytes=8 << 20,
        )
        last_sums = dp_reduce_begin(*last, hop(last[0], "dp", 1))
        last_far = dp_reduce_far(last_sums, bf16, (6, 4))
        w2_far = dp_reduce_far(w2_sums, bf16, (6, 4, 2))
    grad_in, sums1 = [], []
    for i in range(images):
        own, far = parts[i]
        d_in, part = call(
            functools.partial(norm_back_kernel, 0),
            (((rows, width_d), f32), ((8, width_d), f32)),
            own,
            hop(far, "tensor", 2),
            x_own[i],
            d_mids[i],
            small_full,
            nbytes=3 << 20,
        )
        grad_in.append(d_in)
        sums1.append(part)
    outs = jnp.stack(mids) + y_own + y_far.astype(f32) + small_full[5]
    outs = (outs * valid_own).astype(bf16)
    sum1, sum2 = sum(sums1), sum(sums)
    small_sums = jnp.stack(
        [sum1[0], sum2[0], sum1[1], sum2[1], sum2[2], sum2[3], sum2[7], sum2[7]]
    )
    if dp_size == 8:
        w1_own = w1_own.astype(f32)
        w2_own = w2_sums[0] + sum(w2_far)
        small_sums = small_sums + hop(small_sums, "tensor", 1)
        small_sums = small_sums + hop(small_sums, "tensor", 2)
        small_sums = after(small_sums, *last_far, w2_own)
        send, keep = call(
            pack_small,
            (((4, 8, 128), f32),) * 2,
            index,
            small_sums,
            grad_b1[None, :],
            head_bias[None, :],
            scalars=1,
        )
        tiny = keep + hop(send, "dp", 1)
        tiny_far = dp_reduce_far({2 * k: tiny[k] for k in range(4)}, f32, (6, 4, 2))
        last_near = dp_reduce_far(last_sums, bf16, (2,))[0]
        own = last_sums[0] + sum(last_far) + last_near
        wqkv_own = own[:, : 3 * width].reshape(128, 3, width)
        wo_own = jnp.transpose(
            own[:, 3 * width :].reshape(128, width // 128, 128), (1, 0, 2)
        ).reshape(wo.shape)
        got = after(tiny[0], last_near, w1_own) + sum(tiny_far)
        part = got[:6]
        b1_own = got[6].reshape(b1.shape)
        qvb_own = got[7, : qv_bias.size].reshape(qv_bias.shape)
    else:
        scatter = functools.partial(lax.psum_scatter, axis_name="dp", tiled=True)
        w2_own = scatter(grad_w2.astype(f32), scatter_dimension=1)
        w1_own = scatter(grad_w1.astype(f32), scatter_dimension=0)
        wo_own = scatter(grad_wo, scatter_dimension=1)
        wqkv_own = scatter(grad_wqkv, scatter_dimension=0).reshape(wqkv.shape)
        b1_own = scatter(grad_b1.reshape(b1.shape[0], -1), scatter_dimension=1)
        qvb_own = scatter(head_bias.reshape(2, heads, head_dim), scatter_dimension=2)
        part = lax.psum(scatter(small_sums[:6], scatter_dimension=1), "tensor")

    def together(parts):
        return jnp.transpose(parts[:, :slots], (1, 0, 2))

    return (
        together(outs),
        together(jnp.stack(grad_in)),
        wqkv_own.reshape(wqkv.shape),
        qvb_own,
        wo_own,
        w1_own,
        b1_own,
        w2_own,
        part[:2],
        part[2:],
    )


def solution(mesh):
    return jax.shard_map(
        body,
        mesh=mesh,
        in_specs=(
            P("tensor", "dp", None),
            P("dp", None, "tensor"),
            P(None, "tensor", "dp"),
            P("tensor", "dp"),
            P("dp", "tensor"),
            P("tensor", "dp"),
            P("tensor", "dp"),
            P(None, "dp"),
            P(None, "dp"),
            P("tensor", "dp", None),
            P(),
        ),
        out_specs=(
            P("tensor", "dp", None),
            P("tensor", "dp", None),
            P("dp", None, "tensor"),
            P(None, "tensor", "dp"),
            P("tensor", "dp"),
            P("dp", "tensor"),
            P("tensor", "dp"),
            P("tensor", "dp"),
            P(None, "dp"),
            P(None, "dp"),
        ),
        check_vma=False,
    )
```
